256 devices in a mesh: dp: 8 (over z), expert: 32 (over x, y, core).
Axes of the slice: x: 4, y: 4, z: 8, core: 2. Of those that a mesh axis runs over, the one named last changes fastest.
Arguments:
- tokens: bfloat16 [32768, 2048], P(('dp', 'expert')), may hold values from -6 to 6
- out_grad: bfloat16 [32768, 2048], P(('dp', 'expert')), may hold values from -6 to 6
- routes: int32 [32768, 2], P(('dp', 'expert')), may hold values from 0 to 31, all different within a row; in each aligned block of 128 rows (0 to 127, 128 to 255, ...) at most 14 rows name the same one
- gates: float32 [32768, 2], P(('dp', 'expert')), may hold values from 0.2 to 1
- weights: bfloat16 [32, 2048, 2304], P('expert'), may hold values from -0.125 to 0.125
Outputs:
- layer_out: bfloat16 [32768, 2048], P(('dp', 'expert'))
- grad_tokens: bfloat16 [32768, 2048], P(('dp', 'expert'))
- grad_weights: bfloat16 [32, 1024, 2304], P('expert', 'dp')
The draws below stay inside these ranges and needn't reach their ends.
Inputs may be any that keep to these rules, and one draw needn't show every extreme that they name: `routes`: within the 128 tokens of one device, no slot is named by more than 14 of their rows, a bound that some block reaches; a token names 2 different slots.
All inputs are finite; a program needn't handle non-finite values.
Results may differ from the reference program's by a relative error of at most 0.019.
Values may be sent and summed in bfloat16 or wider, within the bound.
No kernel may reach another device: no remote copies, remote signals or barrier semaphores. Data moves between devices by JAX's collectives and lax.ppermute only.
A program may use at most 128 MiB of HBM per device.

```python
import math
import jax
import jax.numpy as jnp
import numpy as np
from jax import lax

D = 2048
FF = 768
TOP = 2
TOK_DEV = 128
SLOTS = 32
CAP = 14
TOKENS = 32768
N_DP = 8
N_EXPERT = 32


def block_scale(key, shape, pieces, smallest, high):
    loudness = 1.0
    for axis_at, blocks in pieces:
        draws = jax.random.uniform(jax.random.fold_in(jax.random.fold_in(key, 6), axis_at), (blocks,), jnp.float32, smallest / len(pieces), high / len(pieces))
        loudness = loudness * jnp.repeat(jnp.exp(draws), shape[axis_at] // blocks).reshape((-1,) + (1,) * (len(shape) - 1 - axis_at))
    return loudness


def assign_block(rng, own, number, rows, number_of, top, bound, slope):
    order = jax.random.permutation(rng, number_of)
    crowded, ordinary = portions_of(number_of, rows * top, bound, slope, True), portions_of(number_of, rows * top, bound, slope, False)
    places = jnp.arange(number_of)

    def named(tallies, offset_by):
        used = int((tallies > 0).sum())
        fixed = max(1, used // 4)
        shifted = fixed + (places - fixed + offset_by * (used - fixed)) % max(1, number_of - fixed)
        return jnp.zeros((number_of,), jnp.int32).at[order[jnp.where(places < fixed, places, shifted)]].set(jnp.asarray(tallies, jnp.int32))

    tallies = jnp.where(number % 4 == 0, named(crowded, number // 4), named(ordinary, number - number // 4 - 1))
    mixed = jax.random.permutation(jax.random.fold_in(own, 3), number_of)
    source_of, taker = mixed[0:number_of // 2 * 2:2], mixed[1:number_of // 2 * 2:2]
    room = jnp.minimum(tallies[source_of] - 1, bound - tallies[taker]) // 2
    room = jnp.where((source_of == order[0]) | (taker == order[0]) | (tallies[taker] == 0), 0, jnp.maximum(room, 0))
    shifted = jax.random.randint(jax.random.fold_in(own, 4), (number_of // 2,), 0, 1 << 20) % (room + 1)
    tallies = tallies.at[source_of].add(-shifted).at[taker].add(shifted)
    items = jnp.searchsorted(jnp.cumsum(tallies), jnp.arange(rows * top), side="right").astype(jnp.int32)
    grid = items.reshape(top, rows).T
    grid = grid[jax.random.permutation(jax.random.fold_in(own, 1), rows)]
    offset_by = jax.random.randint(jax.random.fold_in(own, 2), (rows, 1), 0, top)
    return jnp.take_along_axis(grid, (jnp.arange(top)[None, :] + offset_by) % top, axis=1)


def portions_of(count, total, most, skew, full):
    weights = [(1 << 20) // math.isqrt(grade ** skew) + 1 for grade in range(1, count + 1)]
    largest = most if full else min(most, max(-(-total // count), total * weights[0] // sum(weights)))
    least = 1 if total - largest >= count - 1 else 0
    given, spare = [largest] + [least] * (count - 1), total - largest - least * (count - 1)
    while spare > 0:
        free = [i for i in range(1, count) if given[i] < largest] or [i for i in range(1, count) if given[i] < most]
        pool, budget = sum([weights[i] for i in free]), spare
        for i in free:
            extra = min(most - given[i], max(1, budget * weights[i] // pool), spare)
            given[i] = given[i] + extra
            spare = spare - extra
    return np.array(given)


def bell_draw(rng, dims, deviation, bound, cuts=(), kind=jnp.bfloat16):
    result = deviation * jax.random.normal(rng, dims, jnp.float32)
    if cuts:
        result = result * block_scale(rng, dims, cuts, -0.22, 0.18)
    return jnp.clip(result, -bound, bound).astype(kind)


def setup_inputs(seed: int = 0) -> dict:
    keys = jax.random.split(jax.random.key(seed), 6)
    tokens = bell_draw(keys[0], (TOKENS, D), 1.0, 6.0, ((0, 256),))
    out_grad = bell_draw(keys[1], (TOKENS, D), 1.0, 6.0, ((0, 256),))
    routes_keys = jax.random.split(jax.random.fold_in(keys[2], 1), TOKENS // TOK_DEV)
    routes_turns = jax.random.permutation(jax.random.fold_in(keys[2], 3), TOKENS // TOK_DEV)
    routes = jax.vmap(lambda own, number: assign_block(jax.random.fold_in(keys[2], 2), own, number, TOK_DEV, SLOTS, TOP, CAP, 2))(routes_keys, routes_turns).reshape((TOKENS, TOP))
    gates = jnp.clip(0.2 + 0.8 * jax.random.uniform(keys[3], (TOKENS, TOP), jnp.float32) ** block_scale(keys[3], (TOKENS, TOP), ((0, 256),), -0.2, 0.2), 0.2, 1.0)
    weights = bell_draw(keys[4], (SLOTS, D, 3 * FF), D ** -0.5, 0.125, ((0, 32),))
    return dict(tokens=tokens, out_grad=out_grad, routes=routes, gates=gates, weights=weights)


def slot_positions(flat_routes, slot_count):
    onehot = (flat_routes[:, None] == jnp.arange(slot_count, dtype=jnp.int32)[None, :]).astype(jnp.int32)
    before = jnp.cumsum(onehot, axis=0) - onehot
    return jnp.sum(before * onehot, axis=1).astype(jnp.int32)


def forward_rows(weight, rows_x):
    hidden_width = weight.shape[1] // 3
    gate_up = jnp.dot(rows_x, weight[:, :2 * hidden_width], preferred_element_type=jnp.float32)
    gate_pre = gate_up[:, :hidden_width]
    up_pre = gate_up[:, hidden_width:]
    sigmoid_gate = jax.nn.sigmoid(gate_pre)
    active = gate_pre * sigmoid_gate
    hidden = (active * up_pre).astype(jnp.bfloat16)
    rows_y = lax.dot_general(hidden, weight[:, 2 * hidden_width:], (((1,), (1,)), ((), ())), preferred_element_type=jnp.float32).astype(jnp.bfloat16)
    return rows_y, (gate_pre, up_pre, sigmoid_gate, hidden)


def backward_rows(weight, rows_x, rows_dy, kept_state):
    gate_pre, up_pre, sigmoid_gate, hidden = kept_state
    hidden_width = weight.shape[1] // 3
    d_hidden = jnp.dot(rows_dy, weight[:, 2 * hidden_width:], preferred_element_type=jnp.float32)
    d_gate = d_hidden * up_pre * sigmoid_gate * (1.0 + gate_pre * (1.0 - sigmoid_gate))
    d_up = d_hidden * gate_pre * sigmoid_gate
    d_both = jnp.concatenate([d_gate, d_up], axis=1).astype(jnp.bfloat16)
    rows_dx = lax.dot_general(d_both, weight[:, :2 * hidden_width], (((1,), (1,)), ((), ())), preferred_element_type=jnp.float32).astype(jnp.bfloat16)
    grad_in = lax.dot_general(rows_x, d_both, (((0,), (0,)), ((), ())), preferred_element_type=jnp.float32)
    grad_down = lax.dot_general(rows_dy, hidden, (((0,), (0,)), ((), ())), preferred_element_type=jnp.float32)
    return rows_dx, jnp.concatenate([grad_in, grad_down], axis=1)


def reference(tokens, out_grad, routes, gates, weights):
    devices = N_DP * N_EXPERT
    rows_dev = TOK_DEV * TOP
    total_rows = devices * rows_dev
    blocks = routes.reshape(devices, rows_dev).astype(jnp.int32)
    where_pos = jax.vmap(lambda one_block: slot_positions(one_block, N_EXPERT))(blocks)
    device_id = jnp.arange(devices, dtype=jnp.int32)[:, None]
    dp_id = device_id // N_EXPERT
    source_id = device_id % N_EXPERT
    global_row = device_id * rows_dev + jnp.arange(rows_dev, dtype=jnp.int32)[None, :]
    flat_place = (((blocks * N_DP + dp_id) * N_EXPERT + source_id) * CAP + where_pos).reshape(-1)
    slot_table = jnp.full((N_EXPERT * N_DP * N_EXPERT * CAP,), total_rows, jnp.int32)
    slot_table = slot_table.at[flat_place].set(global_row.reshape(-1)).reshape(N_EXPERT, N_DP, N_EXPERT * CAP)
    flat_gates = gates.reshape(-1)

    def one_slot(loop_carry, slot_id):
        weight = weights[slot_id]

        def one_group(dp_group):
            row_index = slot_table[slot_id, dp_group]
            is_live = row_index < total_rows
            safe_row = jnp.minimum(row_index, total_rows - 1)
            token_index = safe_row // TOP
            rows_x = jnp.where(is_live[:, None], tokens[token_index], jnp.zeros((), tokens.dtype))
            gate_row = jnp.where(is_live, flat_gates[safe_row], jnp.zeros((), flat_gates.dtype))
            rows_dy = (gate_row[:, None] * out_grad[token_index].astype(jnp.float32)).astype(jnp.bfloat16)
            rows_y, kept_state = forward_rows(weight, rows_x)
            rows_dx, partial_value = backward_rows(weight, rows_x, rows_dy, kept_state)
            return rows_y, rows_dx, partial_value.astype(jnp.bfloat16)

        rows_y, rows_dx, partials = lax.map(one_group, jnp.arange(N_DP, dtype=jnp.int32))
        total_sum = jnp.sum(partials.astype(jnp.float32), axis=0)
        return loop_carry, (rows_y, rows_dx, total_sum)

    _, (all_y, all_dx, totals) = lax.scan(one_slot, jnp.zeros((), jnp.int32), jnp.arange(N_EXPERT, dtype=jnp.int32))
    y_rows = all_y.reshape(-1, D)[flat_place].reshape(TOKENS, TOP, D).astype(jnp.float32)
    layer_out = jnp.sum(gates[:, :, None] * y_rows, axis=1).astype(jnp.bfloat16)
    dx_rows = all_dx.reshape(-1, D)[flat_place].reshape(TOKENS, TOP, D).astype(jnp.float32)
    grad_tokens = jnp.sum(dx_rows, axis=1).astype(jnp.bfloat16)
    partner = (jnp.arange(N_EXPERT, dtype=jnp.int32) + N_EXPERT // 2) % N_EXPERT
    combined = (totals + totals[partner]).reshape(N_EXPERT, 2, D // 2, 3 * FF)
    upper_half = (jnp.arange(N_EXPERT) >= N_EXPERT // 2)[:, None, None]
    grad_weights = jnp.where(upper_half, combined[:, 1], combined[:, 0]).astype(jnp.bfloat16)
    return layer_out, grad_tokens, grad_weights
```

```python
import jax
import jax.numpy as jnp
from jax import lax
from jax.experimental import pallas as pl
from jax.experimental.pallas import tpu as pltpu
from jax.sharding import PartitionSpec as P

BF16 = jnp.bfloat16
F32 = jnp.float32
ROWS = 16
VMEM_LIMIT = 58 * 1024 * 1024


def dot(a, b, dims):
    return lax.dot_general(a, b, (dims, ((), ())), preferred_element_type=F32)


def dispatch_mask(routes, slots):
    top, tokens = routes.shape
    slot = lax.broadcasted_iota(jnp.int32, (slots, tokens), 0)
    names = [routes[k : k + 1, :] == slot for k in range(top)]
    named = names[0]
    for one in names[1:]:
        named = named | one
    earlier = (
        lax.broadcasted_iota(jnp.int32, (tokens, tokens), 0)
        < lax.broadcasted_iota(jnp.int32, (tokens, tokens), 1)
    )
    place = dot(
        jnp.where(named, 1.0, 0.0).astype(BF16),
        jnp.where(earlier, 1.0, 0.0).astype(BF16),
        ((1,), (0,)),
    ).astype(jnp.int32)
    place = jnp.where(named, place, ROWS)
    at = lax.broadcasted_iota(jnp.int32, (slots, ROWS, tokens), 1)
    return names, place[:, None, :] == at


def slot_gates(names, gates):
    total = jnp.where(names[0], gates[0:1, :], 0.0)
    for k in range(1, len(names)):
        total = total + jnp.where(names[k], gates[k : k + 1, :], 0.0)
    return total


def pack_kernel(routes_ref, gates_ref, tokens_ref, out_grad_ref, send_ref):
    slots, _, width = send_ref.shape
    names, mask = dispatch_mask(routes_ref[...], slots)
    weight = slot_gates(names, gates_ref[...])
    row_gate = jnp.sum(jnp.where(mask, weight[:, None, :], 0.0), axis=2, keepdims=True)
    pick = jnp.where(mask, 1.0, 0.0).reshape(slots * ROWS, -1).astype(BF16)
    step = 512
    for c in range(0, width, step):
        cols = slice(c, c + step)
        x = dot(pick, tokens_ref[:, cols], ((1,), (0,)))
        send_ref[:, :ROWS, cols] = x.astype(BF16).reshape(slots, ROWS, step)
        g = dot(pick, out_grad_ref[:, cols], ((1,), (0,))).reshape(slots, ROWS, step)
        send_ref[:, ROWS:, cols] = (row_gate * g).astype(BF16)


def grads_kernel(rows_ref, g_ref, u_ref, v_ref, partial_ref, qg_ref, qu_ref, h_ref):
    slots, _, width = rows_ref.shape
    rows = slots * ROWS
    x = rows_ref[:, :ROWS, :].reshape(rows, width)
    dy = rows_ref[:, ROWS:, :].reshape(rows, width)
    a = dot(x, g_ref[...], ((1,), (0,)))
    b = dot(x, u_ref[...], ((1,), (0,)))
    e = dot(dy, v_ref[...], ((1,), (0,)))
    s = jax.nn.sigmoid(a)
    active = a * s
    h = (active * b).astype(BF16)
    qg = (e * b * s * (1.0 + a * (1.0 - s))).astype(BF16)
    qu = (e * active).astype(BF16)
    h_ref[...] = h
    qg_ref[...] = qg
    qu_ref[...] = qu
    chunk = h.shape[1]
    block = partial_ref.shape[0] // 16
    for n, (lhs, rhs) in enumerate(((x, qg), (x, qu), (dy, h))):
        value = dot(lhs, rhs, ((0,), (0,))).astype(BF16)
        for half in range(2):
            for d in range(8):
                partial_ref[
                    pl.ds((2 * d + half) * block, block), pl.ds(n * chunk, chunk)
                ] = value[(half * 8 + d) * block : (half * 8 + d + 1) * block]


def back_kernel(h_ref, qg_ref, qu_ref, w_ref, out_ref):
    slots, _, block = out_ref.shape
    ff = h_ref.shape[1]
    y = dot(h_ref[...], w_ref[:, 2 * ff :], ((1,), (1,)))
    out_ref[:, :ROWS, :] = y.astype(BF16).reshape(slots, ROWS, block)
    dx = dot(qg_ref[...], w_ref[:, :ff], ((1,), (1,)))
    dx = dx + dot(qu_ref[...], w_ref[:, ff : 2 * ff], ((1,), (1,)))
    out_ref[:, ROWS:, :] = dx.astype(BF16).reshape(slots, ROWS, block)


def combine_kernel(routes_ref, gates_ref, back_ref, layer_ref, grad_ref):
    slots, _, width = back_ref.shape
    names, mask = dispatch_mask(routes_ref[...], slots)
    weight = slot_gates(names, gates_ref[...])
    rows = slots * ROWS
    gate = jnp.where(mask, weight[:, None, :], 0.0).reshape(rows, -1)
    high = gate.astype(BF16)
    low = (gate - high.astype(F32)).astype(BF16)
    pick = jnp.where(mask, 1.0, 0.0).reshape(rows, -1).astype(BF16)
    step = 512
    for c in range(0, width, step):
        cols = slice(c, c + step)
        y = back_ref[:, :ROWS, cols].reshape(rows, step)
        value = dot(high, y, ((0,), (0,))) + dot(low, y, ((0,), (0,)))
        layer_ref[:, cols] = value.astype(BF16)
        dx = back_ref[:, ROWS:, cols].reshape(rows, step)
        grad_ref[:, cols] = dot(pick, dx, ((0,), (0,))).astype(BF16)


def join_kernel(which_ref, summed_ref, came_ref, out_ref):
    half, columns = came_ref.shape
    chunk = 256
    steps = columns // chunk // 3
    own = summed_ref[pl.ds(pl.multiple_of(which_ref[0] * half, half), half), :]
    total = (own.astype(F32) + came_ref[...].astype(F32)).astype(BF16)
    for j in range(steps):
        for n in range(3):
            old, new = (3 * j + n) * chunk, (n * steps + j) * chunk
            out_ref[0, :, new : new + chunk] = total[:, old : old + chunk]


def params():
    return pltpu.CompilerParams(vmem_limit_bytes=VMEM_LIMIT)


def cost(flops, moved):
    return pl.CostEstimate(flops=flops, bytes_accessed=moved, transcendentals=0)


def local(tokens, out_grad, routes, gates, weights):
    slots = lax.axis_size("expert")
    groups = lax.axis_size("dp")
    count, width = tokens.shape
    weight = weights[0]
    ff = weight.shape[1] // 3
    rows = slots * ROWS
    chunk = 256
    steps = ff // chunk
    routes_t = routes.T
    gates_t = gates.T
    pair = jax.ShapeDtypeStruct((slots, 2 * ROWS, width), BF16)
    sent = pl.pallas_call(
        pack_kernel,
        out_shape=pair,
        compiler_params=params(),
        cost_estimate=cost(4 * rows * count * width, 6 * rows * width),
        name="pack",
    )(routes_t, gates_t, tokens, out_grad)
    came = lax.all_to_all(sent, "expert", split_axis=0, concat_axis=0, tiled=True)
    row_spec = pl.BlockSpec((rows, chunk), lambda j: (0, j))
    partial, qg, qu, h = pl.pallas_call(
        grads_kernel,
        grid=(steps,),
        in_specs=[
            pl.BlockSpec((slots, 2 * ROWS, width), lambda j: (0, 0, 0)),
            pl.BlockSpec((width, chunk), lambda j: (0, j)),
            pl.BlockSpec((width, chunk), lambda j: (0, steps + j)),
            pl.BlockSpec((width, chunk), lambda j: (0, 2 * steps + j)),
        ],
        out_specs=[
            pl.BlockSpec((width, 3 * chunk), lambda j: (0, j)),
            row_spec,
            row_spec,
            row_spec,
        ],
        out_shape=[jax.ShapeDtypeStruct((width, 3 * ff), BF16)]
        + [jax.ShapeDtypeStruct((rows, ff), BF16)] * 3,
        compiler_params=params(),
        cost_estimate=cost(12 * rows * width * ff, 24 * width * ff),
        name="grads",
    )(came, weight, weight, weight)
    summed = lax.psum_scatter(partial, "dp", scatter_dimension=0, tiled=True)
    block = 256
    whole = pl.BlockSpec((rows, ff), lambda j: (0, 0))
    back = pl.pallas_call(
        back_kernel,
        grid=(width // block,),
        in_specs=[whole, whole, whole, pl.BlockSpec((block, 3 * ff), lambda j: (j, 0))],
        out_specs=pl.BlockSpec((slots, 2 * ROWS, block), lambda j: (0, 0, j)),
        out_shape=pair,
        compiler_params=params(),
        cost_estimate=cost(6 * rows * width * ff, 12 * width * ff),
        name="back",
    )(h, qg, qu, weight)
    home = lax.all_to_all(back, "expert", split_axis=0, concat_axis=0, tiled=True)
    layer_out, grad_tokens = pl.pallas_call(
        combine_kernel,
        out_shape=[jax.ShapeDtypeStruct((count, width), BF16)] * 2,
        compiler_params=params(),
        cost_estimate=cost(6 * rows * count * width, 6 * rows * width),
        name="combine",
    )(routes_t, gates_t, home)
    half = width // 2 // groups
    upper = (lax.axis_index("expert") >= slots // 2).astype(jnp.int32)
    other = lax.dynamic_slice_in_dim(summed, (1 - upper) * half, half, 0)
    route = [((i + slots // 2) % slots, i) for i in range(slots)]
    came_half = lax.ppermute(other, "expert", route)
    total = pl.pallas_call(
        join_kernel,
        in_specs=[pl.BlockSpec(memory_space=pltpu.SMEM)] + [pl.BlockSpec(memory_space=pltpu.VMEM)] * 2,
        out_shape=jax.ShapeDtypeStruct((1, half, 3 * ff), BF16),
        compiler_params=params(),
        name="join",
    )(upper.reshape(1), summed, came_half)
    return (layer_out, grad_tokens, total)


def solution(mesh):
    placed = (
        P(("dp", "expert"), None),
        P(("dp", "expert"), None),
        P(("dp", "expert"), None),
        P(("dp", "expert"), None),
        P("expert", None, None),
    )
    return jax.shard_map(
        local,
        mesh=mesh,
        in_specs=placed,
        out_specs=(P(("dp", "expert"), None), P(("dp", "expert"), None), P("expert", "dp", None)),
        check_vma=False,
    )
```

```python
import functools

import jax
import jax.numpy as jnp
from jax import lax
from jax.experimental import pallas as pl
from jax.experimental.pallas import tpu as pltpu
from jax.sharding import PartitionSpec as P

BF16 = jnp.bfloat16
F32 = jnp.float32
ROWS = 16


def dot(a, b, dims):
    return lax.dot_general(a, b, (dims, ((), ())), preferred_element_type=F32)


def dispatch_mask(routes, slots):
    top, tokens = routes.shape
    slot = lax.broadcasted_iota(jnp.int32, (slots, tokens), 0)
    names = [routes[k : k + 1, :] == slot for k in range(top)]
    named = names[0]
    for one in names[1:]:
        named = named | one
    earlier = (
        lax.broadcasted_iota(jnp.int32, (tokens, tokens), 0)
        < lax.broadcasted_iota(jnp.int32, (tokens, tokens), 1)
    )
    place = dot(
        jnp.where(named, 1.0, 0.0).astype(BF16),
        jnp.where(earlier, 1.0, 0.0).astype(BF16),
        ((1,), (0,)),
    ).astype(jnp.int32)
    place = jnp.where(named, place, ROWS)
    at = lax.broadcasted_iota(jnp.int32, (slots, ROWS, tokens), 1)
    return names, place[:, None, :] == at


def slot_gates(names, gates):
    total = jnp.where(names[0], gates[0:1, :], 0.0)
    for k in range(1, len(names)):
        total = total + jnp.where(names[k], gates[k : k + 1, :], 0.0)
    return total


def pack_kernel(routes_ref, gates_ref, tokens_ref, out_grad_ref, send_ref, pick_ref, gate_ref):
    slots, _, step = send_ref.shape

    @pl.when(pl.program_id(0) == 0)
    def _():
        names, mask = dispatch_mask(routes_ref[...], slots)
        weight = slot_gates(names, gates_ref[...])
        gate_ref[...] = jnp.sum(jnp.where(mask, weight[:, None, :], 0.0), axis=2, keepdims=True)
        pick_ref[...] = jnp.where(mask, 1.0, 0.0).reshape(slots * ROWS, -1).astype(BF16)

    pick = pick_ref[...]
    x = dot(pick, tokens_ref[...], ((1,), (0,)))
    send_ref[:, :ROWS, :] = x.astype(BF16).reshape(slots, ROWS, step)
    g = dot(pick, out_grad_ref[...], ((1,), (0,))).reshape(slots, ROWS, step)
    send_ref[:, ROWS:, :] = (gate_ref[...] * g).astype(BF16)


def expert_rows(at, rows_ref, w_ref, qg_ref, qu_ref, h_ref):
    chunk = h_ref.shape[1]
    ff = w_ref.shape[1] // 3
    slots, _, width = rows_ref.shape
    rows = slots * ROWS
    x = rows_ref[:, :ROWS, :].reshape(rows, width)
    dy = rows_ref[:, ROWS:, :].reshape(rows, width)
    a = dot(x, w_ref[:, pl.ds(pl.multiple_of(at * chunk, chunk), chunk)], ((1,), (0,)))
    b = dot(x, w_ref[:, pl.ds(pl.multiple_of(ff + at * chunk, chunk), chunk)], ((1,), (0,)))
    e = dot(dy, w_ref[:, pl.ds(pl.multiple_of(2 * ff + at * chunk, chunk), chunk)], ((1,), (0,)))
    s = jax.nn.sigmoid(a)
    active = a * s
    h_ref[...] = (active * b).astype(BF16)
    qg_ref[...] = (e * b * s * (1.0 + a * (1.0 - s))).astype(BF16)
    qu_ref[...] = (e * active).astype(BF16)


def first_kernel(groups, rows_ref, w_ref, partial_ref, qg_ref, qu_ref, h_ref):
    slots, _, width = rows_ref.shape
    rows = slots * ROWS
    part = pl.program_id(1)
    block = width // 2 // groups

    @pl.when(part == 0)
    def _():
        expert_rows(pl.program_id(0) + 1, rows_ref, w_ref, qg_ref, qu_ref, h_ref)

    for n, rhs_ref in enumerate((qg_ref, qu_ref, h_ref)):

        @pl.when(part == n + 1)
        def _(n=n, rhs_ref=rhs_ref):
            begin = ROWS if n == 2 else 0
            lhs = rows_ref[:, begin : begin + ROWS, :].reshape(rows, width)
            value = dot(lhs, rhs_ref[...], ((0,), (0,))).astype(BF16)
            for half in range(2):
                for d in range(groups):
                    old, new = (half * groups + d) * block, (2 * d + half) * block
                    partial_ref[new : new + block] = value[old : old + block]


def second_kernel(
    which_ref, rows_ref, w_ref, own_ref, sent_ref, qg_ref, qu_ref, h_ref
):
    slots, _, width = rows_ref.shape
    rows, half = slots * ROWS, width // 2
    part = pl.program_id(0)

    @pl.when(part == 0)
    def _():
        expert_rows(0, rows_ref, w_ref, qg_ref, qu_ref, h_ref)

    for n, rhs_ref in enumerate((qg_ref, qu_ref, h_ref)):

        @pl.when(part == n + 1)
        def _(n=n, rhs_ref=rhs_ref):
            begin = ROWS if n == 2 else 0
            for out_ref, which in ((own_ref, which_ref[0]), (sent_ref, 1 - which_ref[0])):
                cols = pl.ds(pl.multiple_of(which * half, half), half)
                lhs = rows_ref[:, begin : begin + ROWS, cols].reshape(rows, half)
                out_ref[...] = dot(lhs, rhs_ref[...], ((0,), (0,))).astype(BF16)


def back_kernel(h0_ref, qg0_ref, qu0_ref, h_ref, qg_ref, qu_ref, w_ref, out_ref):
    slots, _, block = out_ref.shape
    chunk = h0_ref.shape[1]
    ff = w_ref.shape[1] // 3
    lines = pl.ds(pl.multiple_of(pl.program_id(0) * block, block), block)

    def product(first_ref, rest_ref, base):
        value = dot(first_ref[...], w_ref[lines, base : base + chunk], ((1,), (1,)))
        return value + dot(rest_ref[...], w_ref[lines, base + chunk : base + ff], ((1,), (1,)))

    y = product(h0_ref, h_ref, 2 * ff)
    out_ref[:, :ROWS, :] = y.astype(BF16).reshape(slots, ROWS, block)
    dx = product(qg0_ref, qg_ref, 0) + product(qu0_ref, qu_ref, ff)
    out_ref[:, ROWS:, :] = dx.astype(BF16).reshape(slots, ROWS, block)


def combine_kernel(routes_ref, gates_ref, back_ref, layer_ref, grad_ref):
    slots, _, width = back_ref.shape
    names, mask = dispatch_mask(routes_ref[...], slots)
    weight = slot_gates(names, gates_ref[...])
    rows = slots * ROWS
    gate = jnp.where(mask, weight[:, None, :], 0.0).reshape(rows, -1)
    high = gate.astype(BF16)
    low = (gate - high.astype(F32)).astype(BF16)
    pick = jnp.where(mask, 1.0, 0.0).reshape(rows, -1).astype(BF16)
    step = 512
    for c in range(0, width, step):
        cols = slice(c, c + step)
        y = back_ref[:, :ROWS, cols].reshape(rows, step)
        value = dot(high, y, ((0,), (0,))) + dot(low, y, ((0,), (0,)))
        layer_ref[:, cols] = value.astype(BF16)
        dx = back_ref[:, ROWS:, cols].reshape(rows, step)
        grad_ref[:, cols] = dot(pick, dx, ((0,), (0,))).astype(BF16)


def join_kernel(which_ref, early_ref, came_ref, late_ref, out_ref):
    half, columns = came_ref.shape
    chunk = late_ref.shape[1] // 3
    steps = columns // (3 * chunk) + 1
    own = early_ref[pl.ds(pl.multiple_of(which_ref[0] * half, half), half), :]
    total = (own.astype(F32) + came_ref[...].astype(F32)).astype(BF16)
    for n in range(3):
        base = n * steps * chunk
        out_ref[0, :, base : base + chunk] = late_ref[:, n * chunk : (n + 1) * chunk]
        for j in range(1, steps):
            old, new = (3 * (j - 1) + n) * chunk, base + j * chunk
            out_ref[0, :, new : new + chunk] = total[:, old : old + chunk]


def params(mib):
    return pltpu.CompilerParams(vmem_limit_bytes=mib * 1024 * 1024)


def cost(flops, moved):
    return pl.CostEstimate(flops=flops, bytes_accessed=moved, transcendentals=0)


def local(tokens, out_grad, routes, gates, weights):
    slots = lax.axis_size("expert")
    groups = lax.axis_size("dp")
    count, width = tokens.shape
    top = routes.shape[1]
    weight = weights[0]
    ff = weight.shape[1] // 3
    rows = slots * ROWS
    chunk = 256
    steps = ff // chunk
    half = width // 2
    routes_t = routes.T
    gates_t = gates.T
    upper = (lax.axis_index("expert") >= slots // 2).astype(jnp.int32)
    which = upper.reshape(1)
    smem = pl.BlockSpec(memory_space=pltpu.SMEM)
    vmem = pl.BlockSpec(memory_space=pltpu.VMEM)
    pair = pltpu.HBM((slots, 2 * ROWS, width), BF16)
    step = 512
    sent = pl.pallas_call(
        pack_kernel,
        grid=(width // step,),
        in_specs=[
            pl.BlockSpec((top, count), lambda c: (0, 0)),
            pl.BlockSpec((top, count), lambda c: (0, 0)),
            pl.BlockSpec((count, step), lambda c: (0, c)),
            pl.BlockSpec((count, step), lambda c: (0, c)),
        ],
        out_specs=pl.BlockSpec((slots, 2 * ROWS, step), lambda c: (0, 0, c)),
        out_shape=pair,
        scratch_shapes=[pltpu.VMEM((rows, count), BF16), pltpu.VMEM((slots, ROWS, 1), F32)],
        compiler_params=params(56),
        cost_estimate=cost(4 * rows * count * width, 6 * rows * width),
        name="pack",
    )(routes_t, gates_t, tokens, out_grad)
    came = lax.all_to_all(sent, "expert", split_axis=0, concat_axis=0, tiled=True)

    state = jax.ShapeDtypeStruct((rows, ff - chunk), BF16)
    state_spec = pl.BlockSpec((rows, chunk), lambda j, p: (0, j))
    early, qg, qu, h = pl.pallas_call(
        functools.partial(first_kernel, groups),
        grid=(steps - 1, 4),
        in_specs=[vmem, vmem],
        out_specs=[pl.BlockSpec((width, chunk), lambda j, p: (0, 3 * j + jnp.maximum(p - 1, 0)))]
        + [state_spec] * 3,
        out_shape=[pltpu.HBM((width, 3 * (ff - chunk)), BF16)] + [state] * 3,
        compiler_params=params(24),
        cost_estimate=cost(8 * rows * width * ff, 16 * width * ff),
        name="early_grads",
    )(came, weight)
    early_sum = lax.psum_scatter(early, "dp", scatter_dimension=0, tiled=True)
    state = jax.ShapeDtypeStruct((rows, chunk), BF16)
    state_spec = pl.BlockSpec((rows, chunk), lambda p: (0, 0))
    half_spec = pl.BlockSpec((half, chunk), lambda p: (0, jnp.maximum(p - 1, 0)))
    own, sent_half, qg0, qu0, h0 = pl.pallas_call(
        second_kernel,
        grid=(4,),
        in_specs=[smem, vmem, vmem],
        out_specs=[half_spec] * 2 + [state_spec] * 3,
        out_shape=[pltpu.HBM((half, 3 * chunk), BF16)] * 2 + [state] * 3,
        compiler_params=params(24),
        cost_estimate=cost(4 * rows * width * ff, 8 * width * ff),
        name="late_grads",
    )(which, came, weight)
    route = [((i + slots // 2) % slots, i) for i in range(slots)]
    came_half = lax.ppermute(sent_half, "expert", route)
    block = 512
    back = pl.pallas_call(
        back_kernel,
        grid=(width // block,),
        in_specs=[vmem] * 7,
        out_specs=pl.BlockSpec((slots, 2 * ROWS, block), lambda j: (0, 0, j)),
        out_shape=pair,
        compiler_params=params(24),
        cost_estimate=cost(6 * rows * width * ff, 12 * width * ff),
        name="back",
    )(h0, qg0, qu0, h, qg, qu, weight)
    home = lax.all_to_all(back, "expert", split_axis=0, concat_axis=0, tiled=True)
    late = (own.astype(F32) + came_half.astype(F32)).astype(BF16)
    late_sum = lax.psum_scatter(late, "dp", scatter_dimension=0, tiled=True)
    layer_out, grad_tokens = pl.pallas_call(
        combine_kernel,
        out_shape=[jax.ShapeDtypeStruct((count, width), BF16)] * 2,
        compiler_params=params(24),
        cost_estimate=cost(6 * rows * count * width, 6 * rows * width),
        name="combine",
    )(routes_t, gates_t, home)
    kept = half // groups
    other = lax.dynamic_slice_in_dim(early_sum, (1 - upper) * kept, kept, 0)
    came_early = lax.ppermute(other, "expert", route)
    grad_weights = pl.pallas_call(
        join_kernel,
        in_specs=[smem, vmem, vmem, vmem],
        out_shape=jax.ShapeDtypeStruct((1, kept, 3 * ff), BF16),
        compiler_params=params(8),
        name="join",
    )(which, early_sum, came_early, late_sum)
    return (layer_out, grad_tokens, grad_weights)


def solution(mesh):
    placed = (
        P(("dp", "expert"), None),
        P(("dp", "expert"), None),
        P(("dp", "expert"), None),
        P(("dp", "expert"), None),
        P("expert", None, None),
    )
    return jax.shard_map(
        local,
        mesh=mesh,
        in_specs=placed,
        out_specs=(P(("dp", "expert"), None), P(("dp", "expert"), None), P("expert", "dp", None)),
        check_vma=False,
    )
```

```python
import functools

import jax
import jax.numpy as jnp
from jax import lax
from jax.experimental import pallas as pl
from jax.experimental.pallas import tpu as pltpu
from jax.sharding import PartitionSpec as P

BF16 = jnp.bfloat16
F32 = jnp.float32
ROWS = 16


def dot(a, b, dims):
    return lax.dot_general(a, b, (dims, ((), ())), preferred_element_type=F32)


def dispatch_mask(routes, slots):
    top, tokens = routes.shape
    slot = lax.broadcasted_iota(jnp.int32, (slots, tokens), 0)
    names = [routes[k : k + 1, :] == slot for k in range(top)]
    named = names[0]
    for one in names[1:]:
        named = named | one
    earlier = (
        lax.broadcasted_iota(jnp.int32, (tokens, tokens), 0)
        < lax.broadcasted_iota(jnp.int32, (tokens, tokens), 1)
    )
    place = dot(
        jnp.where(named, 1.0, 0.0).astype(BF16),
        jnp.where(earlier, 1.0, 0.0).astype(BF16),
        ((1,), (0,)),
    ).astype(jnp.int32)
    place = jnp.where(named, place, ROWS)
    at = lax.broadcasted_iota(jnp.int32, (slots, ROWS, tokens), 1)
    return names, place[:, None, :] == at


def slot_gates(names, gates):
    total = jnp.where(names[0], gates[0:1, :], 0.0)
    for k in range(1, len(names)):
        total = total + jnp.where(names[k], gates[k : k + 1, :], 0.0)
    return total


def pack_kernel(routes_ref, gates_ref, tokens_ref, out_grad_ref, send_ref, pick_ref, gate_ref):
    slots, _, step = send_ref.shape

    @pl.when(pl.program_id(0) == 0)
    def _():
        names, mask = dispatch_mask(routes_ref[...], slots)
        weight = slot_gates(names, gates_ref[...])
        gate_ref[...] = jnp.sum(jnp.where(mask, weight[:, None, :], 0.0), axis=2, keepdims=True)
        pick_ref[...] = jnp.where(mask, 1.0, 0.0).reshape(slots * ROWS, -1).astype(BF16)

    pick = pick_ref[...]
    x = dot(pick, tokens_ref[...], ((1,), (0,)))
    send_ref[:, :ROWS, :] = x.astype(BF16).reshape(slots, ROWS, step)
    g = dot(pick, out_grad_ref[...], ((1,), (0,))).reshape(slots, ROWS, step)
    send_ref[:, ROWS:, :] = (gate_ref[...] * g).astype(BF16)


def expert_rows(rows_ref, g, u, v, qg_ref, qu_ref, h_ref):
    slots, _, width = rows_ref.shape
    rows = slots * ROWS
    x = rows_ref[:, :ROWS, :].reshape(rows, width)
    dy = rows_ref[:, ROWS:, :].reshape(rows, width)
    a = dot(x, g, ((1,), (0,)))
    b = dot(x, u, ((1,), (0,)))
    e = dot(dy, v, ((1,), (0,)))
    s = jax.nn.sigmoid(a)
    active = a * s
    h_ref[...] = (active * b).astype(BF16)
    qg_ref[...] = (e * b * s * (1.0 + a * (1.0 - s))).astype(BF16)
    qu_ref[...] = (e * active).astype(BF16)


def early_kernel(plan, groups, rows_ref, w_ref, partial_ref, qg_ref, qu_ref, h_ref):
    slots, _, width = rows_ref.shape
    rows = slots * ROWS
    block = width // 2 // groups
    refs = (qg_ref, qu_ref, h_ref)
    for step, (j, n) in enumerate(plan):

        @pl.when(pl.program_id(0) == step)
        def _(j=j, n=n):
            if n is None:
                chunk, ff = h_ref.shape[1], w_ref.shape[1] // 3
                begins = [n * ff + j * chunk for n in range(3)]
                expert_rows(rows_ref, *(w_ref[:, at : at + chunk] for at in begins), *refs)
                return
            begin = ROWS if n == 2 else 0
            lhs = rows_ref[:, begin : begin + ROWS, :].reshape(rows, width)
            value = dot(lhs, refs[n][...], ((0,), (0,))).astype(BF16)
            for half in range(2):
                for d in range(groups):
                    old, new = (half * groups + d) * block, (2 * d + half) * block
                    partial_ref[new : new + block] = value[old : old + block]


def late_kernel(
    plan,
    which_ref,
    rows_ref,
    g_ref,
    u_ref,
    v_ref,
    kept_ref,
    own_ref,
    sent_ref,
    qg_ref,
    qu_ref,
    h_ref,
):
    slots, _, width = rows_ref.shape
    rows, half = slots * ROWS, width // 2
    refs = (qg_ref, qu_ref, h_ref)
    for step, (j, n) in enumerate(plan):

        @pl.when(pl.program_id(0) == step)
        def _(j=j, n=n):
            if n is None:
                expert_rows(rows_ref, g_ref[...], u_ref[...], v_ref[...], *refs)
                return
            rhs = refs[n][...] if j == 0 else kept_ref[...]
            begin = ROWS if n == 2 else 0
            for out_ref, which in ((own_ref, which_ref[0]), (sent_ref, 1 - which_ref[0])):
                cols = pl.ds(pl.multiple_of(which * half, half), half)
                lhs = rows_ref[:, begin : begin + ROWS, cols].reshape(rows, half)
                out_ref[...] = dot(lhs, rhs, ((0,), (0,))).astype(BF16)


def back_kernel(h0_ref, qg0_ref, qu0_ref, h_ref, qg_ref, qu_ref, w_ref, y_ref, dx_ref):
    slots, _, block = y_ref.shape
    chunk = h0_ref.shape[1]
    ff = w_ref.shape[1] // 3

    def product(first_ref, rest_ref, base):
        value = dot(first_ref[...], w_ref[:, base : base + chunk], ((1,), (1,)))
        return value + dot(rest_ref[...], w_ref[:, base + chunk : base + ff], ((1,), (1,)))

    y = product(h0_ref, h_ref, 2 * ff)
    y_ref[...] = y.astype(BF16).reshape(slots, ROWS, block)
    dx = product(qg0_ref, qg_ref, 0) + product(qu0_ref, qu_ref, ff)
    dx_ref[...] = dx.astype(BF16).reshape(slots, ROWS, block)


def layer_kernel(routes_ref, gates_ref, y_ref, out_ref):
    slots, _, width = y_ref.shape
    names, mask = dispatch_mask(routes_ref[...], slots)
    weight = slot_gates(names, gates_ref[...])
    rows = slots * ROWS
    gate = jnp.where(mask, weight[:, None, :], 0.0).reshape(rows, -1)
    high = gate.astype(BF16)
    low = (gate - high.astype(F32)).astype(BF16)
    step = 512
    for c in range(0, width, step):
        y = y_ref[:, :, c : c + step].reshape(rows, step)
        value = dot(high, y, ((0,), (0,))) + dot(low, y, ((0,), (0,)))
        out_ref[:, c : c + step] = value.astype(BF16)


def tokens_kernel(routes_ref, dx_ref, out_ref):
    slots, _, width = dx_ref.shape
    rows = slots * ROWS
    mask = dispatch_mask(routes_ref[...], slots)[1]
    pick = jnp.where(mask, 1.0, 0.0).reshape(rows, -1).astype(BF16)
    step = 512
    for c in range(0, width, step):
        dx = dx_ref[:, :, c : c + step].reshape(rows, step)
        out_ref[:, c : c + step] = dot(pick, dx, ((0,), (0,))).astype(BF16)


def join_kernel(early_plan, late_plan, which_ref, early_ref, came_ref, late_ref, out_ref):
    half, columns = came_ref.shape
    chunk = columns // len(early_plan)
    steps = out_ref.shape[2] // 3 // chunk
    own = early_ref[pl.ds(pl.multiple_of(which_ref[0] * half, half), half), :]
    total = (own.astype(F32) + came_ref[...].astype(F32)).astype(BF16)
    for plan, value in ((early_plan, total), (late_plan, late_ref[...])):
        for i, (j, n) in enumerate(plan):
            new = (n * steps + j) * chunk
            out_ref[0, :, new : new + chunk] = value[:, i * chunk : (i + 1) * chunk]


def params(mib):
    return pltpu.CompilerParams(vmem_limit_bytes=mib * 1024 * 1024)


def cost(flops, moved):
    return pl.CostEstimate(flops=flops, bytes_accessed=moved, transcendentals=0)


def local(tokens, out_grad, routes, gates, weights):
    slots = lax.axis_size("expert")
    groups = lax.axis_size("dp")
    count, width = tokens.shape
    top = routes.shape[1]
    weight = weights[0]
    ff = weight.shape[1] // 3
    rows = slots * ROWS
    chunk = 256
    steps = ff // chunk
    half = width // 2
    routes_t = routes.T
    gates_t = gates.T
    upper = (lax.axis_index("expert") >= slots // 2).astype(jnp.int32)
    which = upper.reshape(1)
    smem = pl.BlockSpec(memory_space=pltpu.SMEM)
    vmem = pl.BlockSpec(memory_space=pltpu.VMEM)
    pair = pltpu.HBM((slots, 2 * ROWS, width), BF16)
    step = 512
    sent = pl.pallas_call(
        pack_kernel,
        grid=(width // step,),
        in_specs=[
            pl.BlockSpec((top, count), lambda c: (0, 0)),
            pl.BlockSpec((top, count), lambda c: (0, 0)),
            pl.BlockSpec((count, step), lambda c: (0, c)),
            pl.BlockSpec((count, step), lambda c: (0, c)),
        ],
        out_specs=pl.BlockSpec((slots, 2 * ROWS, step), lambda c: (0, 0, c)),
        out_shape=pair,
        scratch_shapes=[pltpu.VMEM((rows, count), BF16), pltpu.VMEM((slots, ROWS, 1), F32)],
        compiler_params=params(24),
        cost_estimate=cost(4 * rows * count * width, 6 * rows * width),
        name="pack",
    )(routes_t, gates_t, tokens, out_grad)
    came = lax.all_to_all(sent, "expert", split_axis=0, concat_axis=0, tiled=True)

    early_plan = ((1, None), (1, 0), (1, 1), (2, None), (2, 0), (2, 1), (2, 2))
    late_plan = ((0, None), (0, 0), (0, 1), (0, 2), (1, 2))
    early_cols = tuple(one for one in early_plan if one[1] is not None)
    late_cols = tuple(one for one in late_plan if one[1] is not None)
    state = jax.ShapeDtypeStruct((rows, ff - chunk), BF16)
    state_spec = pl.BlockSpec((rows, chunk), lambda p: (0, jnp.where(p >= 3, 1, 0)))
    early, qg, qu, h = pl.pallas_call(
        functools.partial(early_kernel, early_plan, groups),
        grid=(len(early_plan),),
        in_specs=[vmem, vmem],
        out_specs=[
            pl.BlockSpec(
                (width, chunk), lambda p: (0, p - jnp.where(p > 0, 1, 0) - jnp.where(p > 3, 1, 0))
            )
        ]
        + [state_spec] * 3,
        out_shape=[pltpu.HBM((width, len(early_cols) * chunk), BF16)] + [state] * 3,
        compiler_params=params(16),
        cost_estimate=cost(8 * rows * width * ff, 16 * width * ff),
        name="early_grads",
    )(came, weight)
    early_sum = lax.psum_scatter(early, "dp", scatter_dimension=0, tiled=True)
    state = jax.ShapeDtypeStruct((rows, chunk), BF16)
    state_spec = pl.BlockSpec((rows, chunk), lambda p: (0, 0))
    half_spec = pl.BlockSpec((half, chunk), lambda p: (0, jnp.maximum(p - 1, 0)))
    own, sent_half, qg0, qu0, h0 = pl.pallas_call(
        functools.partial(late_kernel, late_plan),
        grid=(len(late_plan),),
        in_specs=[smem, pl.BlockSpec((slots, 2 * ROWS, width), lambda p: (0, 0, 0))]
        + [pl.BlockSpec((width, chunk), lambda p, n=n: (0, n * steps)) for n in range(3)]
        + [state_spec],
        out_specs=[half_spec] * 2 + [state_spec] * 3,
        out_shape=[pltpu.HBM((half, len(late_cols) * chunk), BF16)] * 2 + [state] * 3,
        compiler_params=params(50),
        cost_estimate=cost(4 * rows * width * ff, 8 * width * ff),
        name="late_grads",
    )(which, came, weight, weight, weight, h)
    route = [((i + slots // 2) % slots, i) for i in range(slots)]
    came_half = lax.ppermute(sent_half, "expert", route)
    block = 512
    y, dx = pl.pallas_call(
        back_kernel,
        grid=(width // block,),
        in_specs=[pl.BlockSpec((rows, chunk), lambda j: (0, 0))] * 3
        + [pl.BlockSpec((rows, ff - chunk), lambda j: (0, 0))] * 3
        + [pl.BlockSpec((block, 3 * ff), lambda j: (j, 0))],
        out_specs=[pl.BlockSpec((slots, ROWS, block), lambda j: (0, 0, j))] * 2,
        out_shape=[pltpu.HBM((slots, ROWS, width), BF16)] * 2,
        compiler_params=params(50),
        cost_estimate=cost(6 * rows * width * ff, 12 * width * ff),
        name="back",
    )(h0, qg0, qu0, h, qg, qu, weight)
    y = lax.all_to_all(y, "expert", split_axis=0, concat_axis=0, tiled=True)
    y, own = lax.optimization_barrier((y, own))
    dx = lax.all_to_all(dx, "expert", split_axis=0, concat_axis=0, tiled=True)
    late = (own.astype(F32) + came_half.astype(F32)).astype(BF16)
    late_sum = lax.psum_scatter(late, "dp", scatter_dimension=0, tiled=True)
    layer_out = pl.pallas_call(
        layer_kernel,
        out_shape=jax.ShapeDtypeStruct((count, width), BF16),
        compiler_params=params(24),
        cost_estimate=cost(4 * rows * count * width, 3 * rows * width),
        name="layer",
    )(routes_t, gates_t, y)
    grad_tokens = pl.pallas_call(
        tokens_kernel,
        out_shape=jax.ShapeDtypeStruct((count, width), BF16),
        compiler_params=params(24),
        cost_estimate=cost(2 * rows * count * width, 3 * rows * width),
        name="tokens",
    )(routes_t, dx)
    kept = half // groups
    other = lax.dynamic_slice_in_dim(early_sum, (1 - upper) * kept, kept, 0)
    came_early = lax.ppermute(other, "expert", route)
    grad_weights = pl.pallas_call(
        functools.partial(join_kernel, early_cols, late_cols),
        in_specs=[smem, vmem, vmem, vmem],
        out_shape=jax.ShapeDtypeStruct((1, kept, 3 * ff), BF16),
        compiler_params=params(8),
        name="join",
    )(which, early_sum, came_early, late_sum)
    return (layer_out, grad_tokens, grad_weights)


def solution(mesh):
    placed = (
        P(("dp", "expert"), None),
        P(("dp", "expert"), None),
        P(("dp", "expert"), None),
        P(("dp", "expert"), None),
        P("expert", None, None),
    )
    return jax.shard_map(
        local,
        mesh=mesh,
        in_specs=placed,
        out_specs=(P(("dp", "expert"), None), P(("dp", "expert"), None), P("expert", "dp", None)),
        check_vma=False,
    )
```

```python
import functools

import jax
import jax.numpy as jnp
from jax import lax
from jax.experimental import pallas as pl
from jax.experimental.pallas import tpu as pltpu
from jax.sharding import PartitionSpec as P

BF16 = jnp.bfloat16
F32 = jnp.float32
ROWS = 16


def dot(a, b, dims):
    return lax.dot_general(a, b, (dims, ((), ())), preferred_element_type=F32)


def dispatch_mask(routes, slots):
    top, tokens = routes.shape
    slot = lax.broadcasted_iota(jnp.int32, (slots, tokens), 0)
    names = [routes[k : k + 1, :] == slot for k in range(top)]
    named = names[0]
    for one in names[1:]:
        named = named | one
    earlier = (
        lax.broadcasted_iota(jnp.int32, (tokens, tokens), 0)
        < lax.broadcasted_iota(jnp.int32, (tokens, tokens), 1)
    )
    place = dot(
        jnp.where(named, 1.0, 0.0).astype(BF16),
        jnp.where(earlier, 1.0, 0.0).astype(BF16),
        ((1,), (0,)),
    ).astype(jnp.int32)
    place = jnp.where(named, place, ROWS)
    at = lax.broadcasted_iota(jnp.int32, (slots, ROWS, tokens), 1)
    return names, place[:, None, :] == at


def slot_gates(names, gates):
    total = jnp.where(names[0], gates[0:1, :], 0.0)
    for k in range(1, len(names)):
        total = total + jnp.where(names[k], gates[k : k + 1, :], 0.0)
    return total


def pack_kernel(
    routes_hbm,
    gates_hbm,
    tokens_hbm,
    out_grad_hbm,
    send_hbm,
    routes_ref,
    gates_ref,
    tokens_ref,
    out_grad_ref,
    send_ref,
    in_sems,
    out_sems,
):
    slots, _, width = send_ref.shape
    pieces = out_sems.shape[0]
    step = width // pieces
    pairs = (
        (routes_hbm, routes_ref),
        (gates_hbm, gates_ref),
        (tokens_hbm, tokens_ref),
        (out_grad_hbm, out_grad_ref),
    )
    loads = [pltpu.make_async_copy(*pair, in_sems.at[i]) for i, pair in enumerate(pairs)]
    for load in loads:
        load.start()
    loads[0].wait()
    names, mask = dispatch_mask(routes_ref[...], slots)
    pick = jnp.where(mask, 1.0, 0.0).reshape(slots * ROWS, -1).astype(BF16)
    loads[1].wait()
    weight = slot_gates(names, gates_ref[...])
    row_gate = jnp.sum(jnp.where(mask, weight[:, None, :], 0.0), axis=2, keepdims=True)
    loads[2].wait()
    loads[3].wait()
    stores = []
    for piece in range(pieces):
        cols = pl.ds(piece * step, step)
        x = dot(pick, tokens_ref[:, cols], ((1,), (0,)))
        send_ref[:, :ROWS, cols] = x.astype(BF16).reshape(slots, ROWS, step)
        g = dot(pick, out_grad_ref[:, cols], ((1,), (0,))).reshape(slots, ROWS, step)
        send_ref[:, ROWS:, cols] = (row_gate * g).astype(BF16)
        stores.append(
            pltpu.make_async_copy(
                send_ref.at[:, :, cols], send_hbm.at[:, :, cols], out_sems.at[piece]
            )
        )
        stores[-1].start()
    for store in stores:
        store.wait()


def expert_rows(rows_ref, g, u, v, qg_ref, qu_ref, h_ref):
    slots, _, width = rows_ref.shape
    rows = slots * ROWS
    x = rows_ref[:, :ROWS, :].reshape(rows, width)
    dy = rows_ref[:, ROWS:, :].reshape(rows, width)
    a = dot(x, g, ((1,), (0,)))
    b = dot(x, u, ((1,), (0,)))
    e = dot(dy, v, ((1,), (0,)))
    s = jax.nn.sigmoid(a)
    active = a * s
    h_ref[...] = (active * b).astype(BF16)
    qg_ref[...] = (e * b * s * (1.0 + a * (1.0 - s))).astype(BF16)
    qu_ref[...] = (e * active).astype(BF16)


def early_kernel(plan, groups, rows_ref, w_ref, partial_ref, qg_ref, qu_ref, h_ref):
    slots, _, width = rows_ref.shape
    rows = slots * ROWS
    block = width // 2 // groups
    refs = (qg_ref, qu_ref, h_ref)
    for step, (j, n) in enumerate(plan):

        @pl.when(pl.program_id(0) == step)
        def _(j=j, n=n):
            if n is None:
                chunk, ff = h_ref.shape[1], w_ref.shape[1] // 3
                begins = [n * ff + j * chunk for n in range(3)]
                expert_rows(rows_ref, *(w_ref[:, at : at + chunk] for at in begins), *refs)
                return
            begin = ROWS if n == 2 else 0
            lhs = rows_ref[:, begin : begin + ROWS, :].reshape(rows, width)
            value = dot(lhs, refs[n][...], ((0,), (0,))).astype(BF16)
            for half in range(2):
                for d in range(groups):
                    old, new = (half * groups + d) * block, (2 * d + half) * block
                    partial_ref[new : new + block] = value[old : old + block]


def late_kernel(
    plan,
    which_ref,
    rows_ref,
    g_ref,
    u_ref,
    v_ref,
    own_ref,
    sent_ref,
    qg_ref,
    qu_ref,
    h_ref,
):
    slots, _, width = rows_ref.shape
    rows, half = slots * ROWS, width // 2
    refs = (qg_ref, qu_ref, h_ref)
    for step, (j, n) in enumerate(plan):

        @pl.when(pl.program_id(0) == step)
        def _(j=j, n=n):
            if n is None:
                expert_rows(rows_ref, g_ref[...], u_ref[...], v_ref[...], *refs)
                return
            rhs = refs[n][...]
            begin = ROWS if n == 2 else 0
            for out_ref, which in ((own_ref, which_ref[0]), (sent_ref, 1 - which_ref[0])):
                cols = pl.ds(pl.multiple_of(which * half, half), half)
                lhs = rows_ref[:, begin : begin + ROWS, cols].reshape(rows, half)
                out_ref[...] = dot(lhs, rhs, ((0,), (0,))).astype(BF16)


def back_kernel(h0_ref, qg0_ref, qu0_ref, h_ref, qg_ref, qu_ref, w_ref, out_ref):
    slots, _, block = out_ref.shape
    chunk = h0_ref.shape[1]
    ff = w_ref.shape[1] // 3

    def product(first_ref, rest_ref, base):
        value = dot(first_ref[...], w_ref[:, base : base + chunk], ((1,), (1,)))
        return value + dot(rest_ref[...], w_ref[:, base + chunk : base + ff], ((1,), (1,)))

    y = product(h0_ref, h_ref, 2 * ff)
    out_ref[:, :ROWS, :] = y.astype(BF16).reshape(slots, ROWS, block)
    dx = product(qg0_ref, qg_ref, 0) + product(qu0_ref, qu_ref, ff)
    out_ref[:, ROWS:, :] = dx.astype(BF16).reshape(slots, ROWS, block)


def combine_kernel(routes_ref, gates_ref, back_ref, layer_ref, grad_ref):
    slots, _, width = back_ref.shape
    names, mask = dispatch_mask(routes_ref[...], slots)
    weight = slot_gates(names, gates_ref[...])
    rows = slots * ROWS
    gate = jnp.where(mask, weight[:, None, :], 0.0).reshape(rows, -1)
    high = gate.astype(BF16)
    low = (gate - high.astype(F32)).astype(BF16)
    pick = jnp.where(mask, 1.0, 0.0).reshape(rows, -1).astype(BF16)
    step = 512
    for c in range(0, width, step):
        cols = slice(c, c + step)
        y = back_ref[:, :ROWS, cols].reshape(rows, step)
        value = dot(high, y, ((0,), (0,))) + dot(low, y, ((0,), (0,)))
        layer_ref[:, cols] = value.astype(BF16)
        dx = back_ref[:, ROWS:, cols].reshape(rows, step)
        grad_ref[:, cols] = dot(pick, dx, ((0,), (0,))).astype(BF16)


def add_kernel(place_ref, own_ref, came_ref, *out_refs):
    groups, block = len(out_refs), out_refs[0].shape[0]
    for ahead, out_ref in enumerate(out_refs):
        at = lax.rem(place_ref[0] + ahead, groups)
        lines = pl.ds(pl.multiple_of(at * block, block), block)
        out_ref[...] = (own_ref[lines].astype(F32) + came_ref[lines].astype(F32)).astype(BF16)


def join_kernel(early_plan, late_plan, which_ref, early_ref, came_ref, *refs):
    late_refs, out_ref = refs[:-1], refs[-1]
    half, columns = came_ref.shape
    chunk = columns // len(early_plan)
    steps = out_ref.shape[2] // 3 // chunk
    own = early_ref[pl.ds(pl.multiple_of(which_ref[0] * half, half), half), :]
    total = (own.astype(F32) + came_ref[...].astype(F32)).astype(BF16)
    late = late_refs[0][...].astype(F32)
    for late_ref in late_refs[1:]:
        late = late + late_ref[...].astype(F32)
    for plan, value in ((early_plan, total), (late_plan, late.astype(BF16))):
        for i, (j, n) in enumerate(plan):
            new = (n * steps + j) * chunk
            out_ref[0, :, new : new + chunk] = value[:, i * chunk : (i + 1) * chunk]


def params(mib):
    return pltpu.CompilerParams(vmem_limit_bytes=int(mib * 1024 * 1024))


def cost(flops, moved):
    return pl.CostEstimate(flops=flops, bytes_accessed=moved, transcendentals=0)


def local(tokens, out_grad, routes, gates, weights):
    slots = lax.axis_size("expert")
    groups = lax.axis_size("dp")
    count, width = tokens.shape
    top = routes.shape[1]
    weight = weights[0]
    ff = weight.shape[1] // 3
    rows = slots * ROWS
    chunk = 256
    steps = ff // chunk
    half = width // 2
    routes_t = routes.T
    gates_t = gates.T
    upper = (lax.axis_index("expert") >= slots // 2).astype(jnp.int32)
    which = upper.reshape(1)
    smem = pl.BlockSpec(memory_space=pltpu.SMEM)
    vmem = pl.BlockSpec(memory_space=pltpu.VMEM)
    pair = pltpu.HBM((slots, 2 * ROWS, width), BF16)
    hbm = pl.BlockSpec(memory_space=pltpu.HBM)
    sent = pl.pallas_call(
        pack_kernel,
        in_specs=[hbm] * 4,
        out_specs=hbm,
        out_shape=pair,
        scratch_shapes=[
            pltpu.VMEM((top, count), jnp.int32),
            pltpu.VMEM((top, count), F32),
            pltpu.VMEM((count, width), BF16),
            pltpu.VMEM((count, width), BF16),
            pltpu.VMEM((slots, 2 * ROWS, width), BF16),
            pltpu.SemaphoreType.DMA((4,)),
            pltpu.SemaphoreType.DMA((4,)),
        ],
        compiler_params=params(54.2),
        cost_estimate=cost(4 * rows * count * width, 6 * rows * width),
        name="pack",
    )(routes_t, gates_t, tokens, out_grad)
    came = lax.all_to_all(sent, "expert", split_axis=0, concat_axis=0, tiled=True)

    early_plan = ((1, None), (1, 0), (1, 1), (1, 2), (2, None), (2, 0), (2, 1), (2, 2))
    late_plan = ((0, None), (0, 0), (0, 1), (0, 2))
    early_cols = tuple(one for one in early_plan if one[1] is not None)
    late_cols = tuple(one for one in late_plan if one[1] is not None)
    state = pltpu.HBM((rows, ff - chunk), BF16)
    state_spec = pl.BlockSpec((rows, chunk), lambda p: (0, jnp.where(p >= 4, 1, 0)))
    early, qg, qu, h = pl.pallas_call(
        functools.partial(early_kernel, early_plan, groups),
        grid=(len(early_plan),),
        in_specs=[vmem, vmem],
        out_specs=[
            pl.BlockSpec(
                (width, chunk), lambda p: (0, p - jnp.where(p > 0, 1, 0) - jnp.where(p > 4, 1, 0))
            )
        ]
        + [state_spec] * 3,
        out_shape=[pltpu.HBM((width, len(early_cols) * chunk), BF16)] + [state] * 3,
        compiler_params=params(16),
        cost_estimate=cost(8 * rows * width * ff, 16 * width * ff),
        name="early_grads",
    )(came, weight)
    early_sum = lax.psum_scatter(early, "dp", scatter_dimension=0, tiled=True)
    state = pltpu.HBM((rows, chunk), BF16)
    state_spec = pl.BlockSpec((rows, chunk), lambda p: (0, 0))
    half_spec = pl.BlockSpec((half, chunk), lambda p: (0, jnp.maximum(p - 1, 0)))
    own, sent_half, qg0, qu0, h0 = pl.pallas_call(
        functools.partial(late_kernel, late_plan),
        grid=(len(late_plan),),
        in_specs=[smem, pl.BlockSpec((slots, 2 * ROWS, width), lambda p: (0, 0, 0))]
        + [pl.BlockSpec((width, chunk), lambda p, n=n: (0, n * steps)) for n in range(3)],
        out_specs=[half_spec] * 2 + [state_spec] * 3,
        out_shape=[pltpu.HBM((half, len(late_cols) * chunk), BF16)] * 2 + [state] * 3,
        compiler_params=params(50),
        cost_estimate=cost(4 * rows * width * ff, 8 * width * ff),
        name="late_grads",
    )(which, came, weight, weight, weight)
    route = [((i + slots // 2) % slots, i) for i in range(slots)]
    came_half = lax.ppermute(sent_half, "expert", route)
    block = 512
    back = pl.pallas_call(
        back_kernel,
        grid=(width // block,),
        in_specs=[pl.BlockSpec((rows, chunk), lambda j: (0, 0))] * 3
        + [pl.BlockSpec((rows, ff - chunk), lambda j: (0, 0))] * 3
        + [pl.BlockSpec((block, 3 * ff), lambda j: (j, 0))],
        out_specs=pl.BlockSpec((slots, 2 * ROWS, block), lambda j: (0, 0, j)),
        out_shape=pair,
        compiler_params=params(50),
        cost_estimate=cost(6 * rows * width * ff, 12 * width * ff),
        name="back",
    )(h0, qg0, qu0, h, qg, qu, weight)
    home = lax.all_to_all(back, "expert", split_axis=0, concat_axis=0, tiled=True)
    kept = half // groups
    term = jax.ShapeDtypeStruct((kept, len(late_cols) * chunk), BF16)
    late_terms = list(pl.pallas_call(
        add_kernel,
        in_specs=[smem, vmem, vmem],
        out_shape=[term] * groups,
        compiler_params=params(16),
        name="late_sum",
    )(lax.axis_index("dp").reshape(1), own, came_half))
    for ahead in range(1, groups):
        hops = [(i, (i + ahead) % groups) for i in range(groups)]
        late_terms[ahead] = lax.ppermute(late_terms[ahead], "dp", hops)
    layer_out, grad_tokens = pl.pallas_call(
        combine_kernel,
        out_shape=[jax.ShapeDtypeStruct((count, width), BF16)] * 2,
        compiler_params=params(24),
        cost_estimate=cost(6 * rows * count * width, 6 * rows * width),
        name="combine",
    )(routes_t, gates_t, home)
    other = lax.dynamic_slice_in_dim(early_sum, (1 - upper) * kept, kept, 0)
    came_early = lax.ppermute(other, "expert", route)
    grad_weights = pl.pallas_call(
        functools.partial(join_kernel, early_cols, late_cols),
        in_specs=[smem] + [vmem] * (2 + groups),
        out_shape=jax.ShapeDtypeStruct((1, kept, 3 * ff), BF16),
        compiler_params=params(8),
        name="join",
    )(which, early_sum, came_early, *late_terms)
    return (layer_out, grad_tokens, grad_weights)


def solution(mesh):
    placed = (
        P(("dp", "expert"), None),
        P(("dp", "expert"), None),
        P(("dp", "expert"), None),
        P(("dp", "expert"), None),
        P("expert", None, None),
    )
    return jax.shard_map(
        local,
        mesh=mesh,
        in_specs=placed,
        out_specs=(P(("dp", "expert"), None), P(("dp", "expert"), None), P("expert", "dp", None)),
        check_vma=False,
    )
```

```python
import functools

import jax
import jax.numpy as jnp
from jax import lax
from jax.experimental import pallas as pl
from jax.experimental.pallas import tpu as pltpu
from jax.sharding import PartitionSpec as P

BF16 = jnp.bfloat16
F32 = jnp.float32
ROWS = 16


def dot(a, b, dims):
    return lax.dot_general(a, b, (dims, ((), ())), preferred_element_type=F32)


def dispatch_mask(routes, slots):
    top, tokens = routes.shape
    slot = lax.broadcasted_iota(jnp.int32, (slots, tokens), 0)
    names = [routes[k : k + 1, :] == slot for k in range(top)]
    named = names[0]
    for one in names[1:]:
        named = named | one
    earlier = (
        lax.broadcasted_iota(jnp.int32, (tokens, tokens), 0)
        < lax.broadcasted_iota(jnp.int32, (tokens, tokens), 1)
    )
    place = dot(
        jnp.where(named, 1.0, 0.0).astype(BF16),
        jnp.where(earlier, 1.0, 0.0).astype(BF16),
        ((1,), (0,)),
    ).astype(jnp.int32)
    place = jnp.where(named, place, ROWS)
    at = lax.broadcasted_iota(jnp.int32, (slots, ROWS, tokens), 1)
    return names, place[:, None, :] == at


def slot_gates(names, gates):
    total = jnp.where(names[0], gates[0:1, :], 0.0)
    for k in range(1, len(names)):
        total = total + jnp.where(names[k], gates[k : k + 1, :], 0.0)
    return total


def pack_kernel(
    routes_hbm,
    gates_hbm,
    tokens_hbm,
    out_grad_hbm,
    send_hbm,
    routes_ref,
    gates_ref,
    tokens_ref,
    out_grad_ref,
    send_ref,
    in_sems,
    out_sems,
):
    slots, _, width = send_ref.shape
    pieces = out_sems.shape[0]
    step = width // pieces
    pairs = (
        (routes_hbm, routes_ref),
        (gates_hbm, gates_ref),
        (tokens_hbm, tokens_ref),
        (out_grad_hbm, out_grad_ref),
    )
    loads = [pltpu.make_async_copy(*pair, in_sems.at[i]) for i, pair in enumerate(pairs)]
    for load in loads:
        load.start()
    loads[0].wait()
    names, mask = dispatch_mask(routes_ref[...], slots)
    pick = jnp.where(mask, 1.0, 0.0).reshape(slots * ROWS, -1).astype(BF16)
    loads[1].wait()
    weight = slot_gates(names, gates_ref[...])
    row_gate = jnp.sum(jnp.where(mask, weight[:, None, :], 0.0), axis=2, keepdims=True)
    loads[2].wait()
    loads[3].wait()
    stores = []
    for piece in range(pieces):
        cols = pl.ds(piece * step, step)
        x = dot(pick, tokens_ref[:, cols], ((1,), (0,)))
        send_ref[:, :ROWS, cols] = x.astype(BF16).reshape(slots, ROWS, step)
        g = dot(pick, out_grad_ref[:, cols], ((1,), (0,))).reshape(slots, ROWS, step)
        send_ref[:, ROWS:, cols] = (row_gate * g).astype(BF16)
        stores.append(
            pltpu.make_async_copy(
                send_ref.at[:, :, cols], send_hbm.at[:, :, cols], out_sems.at[piece]
            )
        )
        stores[-1].start()
    for store in stores:
        store.wait()


def expert_rows(rows_ref, g, u, v, qg_ref, qu_ref, h_ref):
    slots, _, width = rows_ref.shape
    rows = slots * ROWS
    x = rows_ref[:, :ROWS, :].reshape(rows, width)
    dy = rows_ref[:, ROWS:, :].reshape(rows, width)
    a = dot(x, g, ((1,), (0,)))
    b = dot(x, u, ((1,), (0,)))
    e = dot(dy, v, ((1,), (0,)))
    s = jax.nn.sigmoid(a)
    active = a * s
    h_ref[...] = (active * b).astype(BF16)
    qg_ref[...] = (e * b * s * (1.0 + a * (1.0 - s))).astype(BF16)
    qu_ref[...] = (e * active).astype(BF16)


def early_kernel(plan, groups, rows_ref, w_ref, partial_ref, qg_ref, qu_ref, h_ref):
    slots, _, width = rows_ref.shape
    rows = slots * ROWS
    block = width // 2 // groups
    refs = (qg_ref, qu_ref, h_ref)
    for step, (j, n) in enumerate(plan):

        @pl.when(pl.program_id(0) == step)
        def _(j=j, n=n):
            if n is None:
                chunk, ff = h_ref.shape[1], w_ref.shape[1] // 3
                begins = [n * ff + j * chunk for n in range(3)]
                expert_rows(rows_ref, *(w_ref[:, at : at + chunk] for at in begins), *refs)
                return
            begin = ROWS if n == 2 else 0
            lhs = rows_ref[:, begin : begin + ROWS, :].reshape(rows, width)
            value = dot(lhs, refs[n][...], ((0,), (0,))).astype(BF16)
            for half in range(2):
                for d in range(groups):
                    old, new = (half * groups + d) * block, (2 * d + half) * block
                    partial_ref[new : new + block] = value[old : old + block]


def late_kernel(
    plan,
    which_ref,
    rows_ref,
    g_ref,
    u_ref,
    v_ref,
    own_ref,
    sent_ref,
    qg_ref,
    qu_ref,
    h_ref,
):
    slots, _, width = rows_ref.shape
    rows, half = slots * ROWS, width // 2
    refs = (qg_ref, qu_ref, h_ref)
    for step, (j, n) in enumerate(plan):

        @pl.when(pl.program_id(0) == step)
        def _(j=j, n=n):
            if n is None:
                expert_rows(rows_ref, g_ref[...], u_ref[...], v_ref[...], *refs)
                return
            rhs = refs[n][...]
            begin = ROWS if n == 2 else 0
            for out_ref, which in ((own_ref, which_ref[0]), (sent_ref, 1 - which_ref[0])):
                cols = pl.ds(pl.multiple_of(which * half, half), half)
                lhs = rows_ref[:, begin : begin + ROWS, cols].reshape(rows, half)
                out_ref[...] = dot(lhs, rhs, ((0,), (0,))).astype(BF16)


def back_kernel(h0_ref, qg0_ref, qu0_ref, h_ref, qg_ref, qu_ref, w_ref, out_ref):
    slots, _, block = out_ref.shape
    chunk = h0_ref.shape[1]
    ff = w_ref.shape[1] // 3

    def product(first_ref, rest_ref, base):
        value = dot(first_ref[...], w_ref[:, base : base + chunk], ((1,), (1,)))
        return value + dot(rest_ref[...], w_ref[:, base + chunk : base + ff], ((1,), (1,)))

    y = product(h0_ref, h_ref, 2 * ff)
    out_ref[:, :ROWS, :] = y.astype(BF16).reshape(slots, ROWS, block)
    dx = product(qg0_ref, qg_ref, 0) + product(qu0_ref, qu_ref, ff)
    out_ref[:, ROWS:, :] = dx.astype(BF16).reshape(slots, ROWS, block)


def combine_kernel(routes_ref, gates_ref, back_ref, layer_ref, grad_ref):
    slots, _, width = back_ref.shape
    names, mask = dispatch_mask(routes_ref[...], slots)
    weight = slot_gates(names, gates_ref[...])
    rows = slots * ROWS
    gate = jnp.where(mask, weight[:, None, :], 0.0).reshape(rows, -1)
    high = gate.astype(BF16)
    low = (gate - high.astype(F32)).astype(BF16)
    pick = jnp.where(mask, 1.0, 0.0).reshape(rows, -1).astype(BF16)
    step = 512
    for c in range(0, width, step):
        cols = slice(c, c + step)
        y = back_ref[:, :ROWS, cols].reshape(rows, step)
        value = dot(high, y, ((0,), (0,))) + dot(low, y, ((0,), (0,)))
        layer_ref[:, cols] = value.astype(BF16)
        dx = back_ref[:, ROWS:, cols].reshape(rows, step)
        grad_ref[:, cols] = dot(pick, dx, ((0,), (0,))).astype(BF16)


def join_kernel(early_plan, late_plan, which_ref, early_ref, came_ref, late_ref, out_ref):
    half, columns = came_ref.shape
    chunk = columns // len(early_plan)
    steps = out_ref.shape[2] // 3 // chunk
    own = early_ref[pl.ds(pl.multiple_of(which_ref[0] * half, half), half), :]
    total = (own.astype(F32) + came_ref[...].astype(F32)).astype(BF16)
    for plan, value in ((early_plan, total), (late_plan, late_ref[...])):
        for i, (j, n) in enumerate(plan):
            new = (n * steps + j) * chunk
            out_ref[0, :, new : new + chunk] = value[:, i * chunk : (i + 1) * chunk]


def params(mib):
    return pltpu.CompilerParams(vmem_limit_bytes=int(mib * 1024 * 1024))


def cost(flops, moved):
    return pl.CostEstimate(flops=flops, bytes_accessed=moved, transcendentals=0)


def local(tokens, out_grad, routes, gates, weights):
    slots = lax.axis_size("expert")
    groups = lax.axis_size("dp")
    count, width = tokens.shape
    top = routes.shape[1]
    weight = weights[0]
    ff = weight.shape[1] // 3
    rows = slots * ROWS
    chunk = 256
    steps = ff // chunk
    half = width // 2
    routes_t = routes.T
    gates_t = gates.T
    upper = (lax.axis_index("expert") >= slots // 2).astype(jnp.int32)
    which = upper.reshape(1)
    smem = pl.BlockSpec(memory_space=pltpu.SMEM)
    vmem = pl.BlockSpec(memory_space=pltpu.VMEM)
    pair = pltpu.HBM((slots, 2 * ROWS, width), BF16)
    hbm = pl.BlockSpec(memory_space=pltpu.HBM)
    sent = pl.pallas_call(
        pack_kernel,
        in_specs=[hbm] * 4,
        out_specs=hbm,
        out_shape=pair,
        scratch_shapes=[
            pltpu.VMEM((top, count), jnp.int32),
            pltpu.VMEM((top, count), F32),
            pltpu.VMEM((count, width), BF16),
            pltpu.VMEM((count, width), BF16),
            pltpu.VMEM((slots, 2 * ROWS, width), BF16),
            pltpu.SemaphoreType.DMA((4,)),
            pltpu.SemaphoreType.DMA((4,)),
        ],
        compiler_params=params(54.2),
        cost_estimate=cost(4 * rows * count * width, 6 * rows * width),
        name="pack",
    )(routes_t, gates_t, tokens, out_grad)
    came = lax.all_to_all(sent, "expert", split_axis=0, concat_axis=0, tiled=True)

    early_plan = ((1, None), (1, 0), (1, 1), (1, 2), (2, None), (2, 0), (2, 1), (2, 2))
    late_plan = ((0, None), (0, 0), (0, 1), (0, 2))
    early_cols = tuple(one for one in early_plan if one[1] is not None)
    late_cols = tuple(one for one in late_plan if one[1] is not None)
    state = pltpu.HBM((rows, ff - chunk), BF16)
    state_spec = pl.BlockSpec((rows, chunk), lambda p: (0, jnp.where(p >= 4, 1, 0)))
    early, qg, qu, h = pl.pallas_call(
        functools.partial(early_kernel, early_plan, groups),
        grid=(len(early_plan),),
        in_specs=[vmem, vmem],
        out_specs=[
            pl.BlockSpec(
                (width, chunk), lambda p: (0, p - jnp.where(p > 0, 1, 0) - jnp.where(p > 4, 1, 0))
            )
        ]
        + [state_spec] * 3,
        out_shape=[pltpu.HBM((width, len(early_cols) * chunk), BF16)] + [state] * 3,
        compiler_params=params(16),
        cost_estimate=cost(8 * rows * width * ff, 16 * width * ff),
        name="early_grads",
    )(came, weight)
    early_sum = lax.psum_scatter(early, "dp", scatter_dimension=0, tiled=True)
    state = pltpu.HBM((rows, chunk), BF16)
    state_spec = pl.BlockSpec((rows, chunk), lambda p: (0, 0))
    half_spec = pl.BlockSpec((half, chunk), lambda p: (0, jnp.maximum(p - 1, 0)))
    own, sent_half, qg0, qu0, h0 = pl.pallas_call(
        functools.partial(late_kernel, late_plan),
        grid=(len(late_plan),),
        in_specs=[smem, pl.BlockSpec((slots, 2 * ROWS, width), lambda p: (0, 0, 0))]
        + [pl.BlockSpec((width, chunk), lambda p, n=n: (0, n * steps)) for n in range(3)],
        out_specs=[half_spec] * 2 + [state_spec] * 3,
        out_shape=[pltpu.HBM((half, len(late_cols) * chunk), BF16)] * 2 + [state] * 3,
        compiler_params=params(50),
        cost_estimate=cost(4 * rows * width * ff, 8 * width * ff),
        name="late_grads",
    )(which, came, weight, weight, weight)
    route = [((i + slots // 2) % slots, i) for i in range(slots)]
    came_half = lax.ppermute(sent_half, "expert", route)
    block = 512
    back = pl.pallas_call(
        back_kernel,
        grid=(width // block,),
        in_specs=[pl.BlockSpec((rows, chunk), lambda j: (0, 0))] * 3
        + [pl.BlockSpec((rows, ff - chunk), lambda j: (0, 0))] * 3
        + [pl.BlockSpec((block, 3 * ff), lambda j: (j, 0))],
        out_specs=pl.BlockSpec((slots, 2 * ROWS, block), lambda j: (0, 0, j)),
        out_shape=pair,
        compiler_params=params(50),
        cost_estimate=cost(6 * rows * width * ff, 12 * width * ff),
        name="back",
    )(h0, qg0, qu0, h, qg, qu, weight)
    home = lax.all_to_all(back, "expert", split_axis=0, concat_axis=0, tiled=True)
    late = (own.astype(F32) + came_half.astype(F32)).astype(BF16)
    late_sum = lax.psum_scatter(late, "dp", scatter_dimension=0, tiled=True)
    layer_out, grad_tokens = pl.pallas_call(
        combine_kernel,
        out_shape=[jax.ShapeDtypeStruct((count, width), BF16)] * 2,
        compiler_params=params(24),
        cost_estimate=cost(6 * rows * count * width, 6 * rows * width),
        name="combine",
    )(routes_t, gates_t, home)
    kept = half // groups
    other = lax.dynamic_slice_in_dim(early_sum, (1 - upper) * kept, kept, 0)
    came_early = lax.ppermute(other, "expert", route)
    grad_weights = pl.pallas_call(
        functools.partial(join_kernel, early_cols, late_cols),
        in_specs=[smem, vmem, vmem, vmem],
        out_shape=jax.ShapeDtypeStruct((1, kept, 3 * ff), BF16),
        compiler_params=params(8),
        name="join",
    )(which, early_sum, came_early, late_sum)
    return (layer_out, grad_tokens, grad_weights)


def solution(mesh):
    placed = (
        P(("dp", "expert"), None),
        P(("dp", "expert"), None),
        P(("dp", "expert"), None),
        P(("dp", "expert"), None),
        P("expert", None, None),
    )
    return jax.shard_map(
        local,
        mesh=mesh,
        in_specs=placed,
        out_specs=(P(("dp", "expert"), None), P(("dp", "expert"), None), P("expert", "dp", None)),
        check_vma=False,
    )
```

```python
import functools

import jax
import jax.numpy as jnp
from jax import lax
from jax.experimental import pallas as pl
from jax.experimental.pallas import tpu as pltpu
from jax.sharding import PartitionSpec as P

BF16 = jnp.bfloat16
F32 = jnp.float32
ROWS = 16


def dot(a, b, dims):
    return lax.dot_general(a, b, (dims, ((), ())), preferred_element_type=F32)


def dispatch_mask(routes, slots):
    top, tokens = routes.shape
    slot = lax.broadcasted_iota(jnp.int32, (slots, tokens), 0)
    names = [routes[k : k + 1, :] == slot for k in range(top)]
    named = names[0]
    for one in names[1:]:
        named = named | one
    earlier = (
        lax.broadcasted_iota(jnp.int32, (tokens, tokens), 0)
        < lax.broadcasted_iota(jnp.int32, (tokens, tokens), 1)
    )
    place = dot(
        jnp.where(named, 1.0, 0.0).astype(BF16),
        jnp.where(earlier, 1.0, 0.0).astype(BF16),
        ((1,), (0,)),
    ).astype(jnp.int32)
    place = jnp.where(named, place, ROWS)
    at = lax.broadcasted_iota(jnp.int32, (slots, ROWS, tokens), 1)
    return names, place[:, None, :] == at


def slot_gates(names, gates):
    total = jnp.where(names[0], gates[0:1, :], 0.0)
    for k in range(1, len(names)):
        total = total + jnp.where(names[k], gates[k : k + 1, :], 0.0)
    return total


def pack_kernel(
    routes_hbm,
    gates_hbm,
    tokens_hbm,
    out_grad_hbm,
    send_hbm,
    routes_ref,
    gates_ref,
    tokens_ref,
    out_grad_ref,
    send_ref,
    in_sems,
    out_sems,
):
    slots, _, width = send_ref.shape
    pieces = out_sems.shape[0]
    step = width // pieces
    pairs = (
        (routes_hbm, routes_ref),
        (gates_hbm, gates_ref),
        (tokens_hbm, tokens_ref),
        (out_grad_hbm, out_grad_ref),
    )
    loads = [pltpu.make_async_copy(*pair, in_sems.at[i]) for i, pair in enumerate(pairs)]
    for load in loads:
        load.start()
    loads[0].wait()
    names, mask = dispatch_mask(routes_ref[...], slots)
    pick = jnp.where(mask, 1.0, 0.0).reshape(slots * ROWS, -1).astype(BF16)
    loads[1].wait()
    weight = slot_gates(names, gates_ref[...])
    row_gate = jnp.sum(jnp.where(mask, weight[:, None, :], 0.0), axis=2, keepdims=True)
    loads[2].wait()
    loads[3].wait()
    stores = []
    for piece in range(pieces):
        cols = pl.ds(piece * step, step)
        x = dot(pick, tokens_ref[:, cols], ((1,), (0,)))
        send_ref[:, :ROWS, cols] = x.astype(BF16).reshape(slots, ROWS, step)
        g = dot(pick, out_grad_ref[:, cols], ((1,), (0,))).reshape(slots, ROWS, step)
        send_ref[:, ROWS:, cols] = (row_gate * g).astype(BF16)
        stores.append(
            pltpu.make_async_copy(
                send_ref.at[:, :, cols], send_hbm.at[:, :, cols], out_sems.at[piece]
            )
        )
        stores[-1].start()
    for store in stores:
        store.wait()


def expert_rows(rows_ref, g, u, v, qg_ref, qu_ref, h_ref):
    slots, _, width = rows_ref.shape
    rows = slots * ROWS
    x = rows_ref[:, :ROWS, :].reshape(rows, width)
    dy = rows_ref[:, ROWS:, :].reshape(rows, width)
    a = dot(x, g, ((1,), (0,)))
    b = dot(x, u, ((1,), (0,)))
    e = dot(dy, v, ((1,), (0,)))
    s = jax.nn.sigmoid(a)
    active = a * s
    h_ref[...] = (active * b).astype(BF16)
    qg_ref[...] = (e * b * s * (1.0 + a * (1.0 - s))).astype(BF16)
    qu_ref[...] = (e * active).astype(BF16)


def early_kernel(plan, groups, rows_ref, w_ref, partial_ref, qg_ref, qu_ref, h_ref):
    slots, _, width = rows_ref.shape
    rows = slots * ROWS
    block = width // 2 // groups
    refs = (qg_ref, qu_ref, h_ref)
    for step, (j, n) in enumerate(plan):

        @pl.when(pl.program_id(0) == step)
        def _(j=j, n=n):
            if n is None:
                chunk, ff = h_ref.shape[1], w_ref.shape[1] // 3
                begins = [n * ff + j * chunk for n in range(3)]
                expert_rows(rows_ref, *(w_ref[:, at : at + chunk] for at in begins), *refs)
                return
            begin = ROWS if n == 2 else 0
            lhs = rows_ref[:, begin : begin + ROWS, :].reshape(rows, width)
            value = dot(lhs, refs[n][...], ((0,), (0,))).astype(BF16)
            for half in range(2):
                for d in range(groups):
                    old, new = (half * groups + d) * block, (2 * d + half) * block
                    partial_ref[new : new + block] = value[old : old + block]


def late_kernel(
    plan,
    which_ref,
    rows_ref,
    g_ref,
    u_ref,
    v_ref,
    kept_ref,
    own_ref,
    sent_ref,
    qg_ref,
    qu_ref,
    h_ref,
):
    slots, _, width = rows_ref.shape
    rows, half = slots * ROWS, width // 2
    refs = (qg_ref, qu_ref, h_ref)
    for step, (j, n) in enumerate(plan):

        @pl.when(pl.program_id(0) == step)
        def _(j=j, n=n):
            if n is None:
                expert_rows(rows_ref, g_ref[...], u_ref[...], v_ref[...], *refs)
                return
            rhs = refs[n][...] if j == 0 else kept_ref[...]
            begin = ROWS if n == 2 else 0
            for out_ref, which in ((own_ref, which_ref[0]), (sent_ref, 1 - which_ref[0])):
                cols = pl.ds(pl.multiple_of(which * half, half), half)
                lhs = rows_ref[:, begin : begin + ROWS, cols].reshape(rows, half)
                out_ref[...] = dot(lhs, rhs, ((0,), (0,))).astype(BF16)


def back_kernel(h0_ref, qg0_ref, qu0_ref, h_ref, qg_ref, qu_ref, w_ref, out_ref):
    slots, _, block = out_ref.shape
    chunk = h0_ref.shape[1]
    ff = w_ref.shape[1] // 3

    def product(first_ref, rest_ref, base):
        value = dot(first_ref[...], w_ref[:, base : base + chunk], ((1,), (1,)))
        return value + dot(rest_ref[...], w_ref[:, base + chunk : base + ff], ((1,), (1,)))

    y = product(h0_ref, h_ref, 2 * ff)
    out_ref[:, :ROWS, :] = y.astype(BF16).reshape(slots, ROWS, block)
    dx = product(qg0_ref, qg_ref, 0) + product(qu0_ref, qu_ref, ff)
    out_ref[:, ROWS:, :] = dx.astype(BF16).reshape(slots, ROWS, block)


def combine_kernel(routes_ref, gates_ref, back_ref, layer_ref, grad_ref):
    slots, _, width = back_ref.shape
    names, mask = dispatch_mask(routes_ref[...], slots)
    weight = slot_gates(names, gates_ref[...])
    rows = slots * ROWS
    gate = jnp.where(mask, weight[:, None, :], 0.0).reshape(rows, -1)
    high = gate.astype(BF16)
    low = (gate - high.astype(F32)).astype(BF16)
    pick = jnp.where(mask, 1.0, 0.0).reshape(rows, -1).astype(BF16)
    step = 512
    for c in range(0, width, step):
        cols = slice(c, c + step)
        y = back_ref[:, :ROWS, cols].reshape(rows, step)
        value = dot(high, y, ((0,), (0,))) + dot(low, y, ((0,), (0,)))
        layer_ref[:, cols] = value.astype(BF16)
        dx = back_ref[:, ROWS:, cols].reshape(rows, step)
        grad_ref[:, cols] = dot(pick, dx, ((0,), (0,))).astype(BF16)


def other_kernel(which_ref, summed_ref, out_ref):
    half = out_ref.shape[0]
    begin = pl.multiple_of((1 - which_ref[0]) * half, half)
    out_ref[...] = summed_ref[pl.ds(begin, half), :]


def join_kernel(early_plan, late_plan, which_ref, early_ref, came_ref, late_ref, out_ref):
    half, columns = came_ref.shape
    chunk = columns // len(early_plan)
    steps = out_ref.shape[2] // 3 // chunk
    own = early_ref[pl.ds(pl.multiple_of(which_ref[0] * half, half), half), :]
    total = (own.astype(F32) + came_ref[...].astype(F32)).astype(BF16)
    for plan, value in ((early_plan, total), (late_plan, late_ref[...])):
        for i, (j, n) in enumerate(plan):
            new = (n * steps + j) * chunk
            out_ref[0, :, new : new + chunk] = value[:, i * chunk : (i + 1) * chunk]


def params(mib):
    return pltpu.CompilerParams(vmem_limit_bytes=int(mib * 1024 * 1024))


def cost(flops, moved):
    return pl.CostEstimate(flops=flops, bytes_accessed=moved, transcendentals=0)


def local(tokens, out_grad, routes, gates, weights):
    slots = lax.axis_size("expert")
    groups = lax.axis_size("dp")
    count, width = tokens.shape
    top = routes.shape[1]
    weight = weights[0]
    ff = weight.shape[1] // 3
    rows = slots * ROWS
    chunk = 256
    steps = ff // chunk
    half = width // 2
    routes_t = routes.T
    gates_t = gates.T
    upper = (lax.axis_index("expert") >= slots // 2).astype(jnp.int32)
    which = upper.reshape(1)
    smem = pl.BlockSpec(memory_space=pltpu.SMEM)
    vmem = pl.BlockSpec(memory_space=pltpu.VMEM)
    pair = pltpu.HBM((slots, 2 * ROWS, width), BF16)
    hbm = pl.BlockSpec(memory_space=pltpu.HBM)
    sent = pl.pallas_call(
        pack_kernel,
        in_specs=[hbm] * 4,
        out_specs=hbm,
        out_shape=pair,
        scratch_shapes=[
            pltpu.VMEM((top, count), jnp.int32),
            pltpu.VMEM((top, count), F32),
            pltpu.VMEM((count, width), BF16),
            pltpu.VMEM((count, width), BF16),
            pltpu.VMEM((slots, 2 * ROWS, width), BF16),
            pltpu.SemaphoreType.DMA((4,)),
            pltpu.SemaphoreType.DMA((4,)),
        ],
        compiler_params=params(54.2),
        cost_estimate=cost(4 * rows * count * width, 6 * rows * width),
        name="pack",
    )(routes_t, gates_t, tokens, out_grad)
    came = lax.all_to_all(sent, "expert", split_axis=0, concat_axis=0, tiled=True)

    early_plan = ((1, None), (1, 0), (1, 1), (2, None), (2, 0), (2, 1), (2, 2))
    late_plan = ((0, None), (0, 0), (0, 1), (0, 2), (1, 2))
    early_cols = tuple(one for one in early_plan if one[1] is not None)
    late_cols = tuple(one for one in late_plan if one[1] is not None)
    state = pltpu.HBM((rows, ff - chunk), BF16)
    state_spec = pl.BlockSpec((rows, chunk), lambda p: (0, jnp.where(p >= 3, 1, 0)))
    early, qg, qu, h = pl.pallas_call(
        functools.partial(early_kernel, early_plan, groups),
        grid=(len(early_plan),),
        in_specs=[vmem, vmem],
        out_specs=[
            pl.BlockSpec(
                (width, chunk), lambda p: (0, p - jnp.where(p > 0, 1, 0) - jnp.where(p > 3, 1, 0))
            )
        ]
        + [state_spec] * 3,
        out_shape=[pltpu.HBM((width, len(early_cols) * chunk), BF16)] + [state] * 3,
        compiler_params=params(16),
        cost_estimate=cost(8 * rows * width * ff, 16 * width * ff),
        name="early_grads",
    )(came, weight)
    early_sum = lax.psum_scatter(early, "dp", scatter_dimension=0, tiled=True)
    state = pltpu.HBM((rows, chunk), BF16)
    state_spec = pl.BlockSpec((rows, chunk), lambda p: (0, 0))
    half_spec = pl.BlockSpec((half, chunk), lambda p: (0, jnp.maximum(p - 1, 0)))
    own, sent_half, qg0, qu0, h0 = pl.pallas_call(
        functools.partial(late_kernel, late_plan),
        grid=(len(late_plan),),
        in_specs=[smem, pl.BlockSpec((slots, 2 * ROWS, width), lambda p: (0, 0, 0))]
        + [pl.BlockSpec((width, chunk), lambda p, n=n: (0, n * steps)) for n in range(3)]
        + [state_spec],
        out_specs=[half_spec] * 2 + [state_spec] * 3,
        out_shape=[pltpu.HBM((half, len(late_cols) * chunk), BF16)] * 2 + [state] * 3,
        compiler_params=params(50),
        cost_estimate=cost(4 * rows * width * ff, 8 * width * ff),
        name="late_grads",
    )(which, came, weight, weight, weight, h)
    route = [((i + slots // 2) % slots, i) for i in range(slots)]
    came_half = lax.ppermute(sent_half, "expert", route)
    block = 512
    back = pl.pallas_call(
        back_kernel,
        grid=(width // block,),
        in_specs=[pl.BlockSpec((rows, chunk), lambda j: (0, 0))] * 3
        + [pl.BlockSpec((rows, ff - chunk), lambda j: (0, 0))] * 3
        + [pl.BlockSpec((block, 3 * ff), lambda j: (j, 0))],
        out_specs=pl.BlockSpec((slots, 2 * ROWS, block), lambda j: (0, 0, j)),
        out_shape=pair,
        compiler_params=params(50),
        cost_estimate=cost(6 * rows * width * ff, 12 * width * ff),
        name="back",
    )(h0, qg0, qu0, h, qg, qu, weight)
    home = lax.all_to_all(back, "expert", split_axis=0, concat_axis=0, tiled=True)
    late = (own.astype(F32) + came_half.astype(F32)).astype(BF16)
    late_sum = lax.psum_scatter(late, "dp", scatter_dimension=0, tiled=True)
    layer_out, grad_tokens = pl.pallas_call(
        combine_kernel,
        out_shape=[jax.ShapeDtypeStruct((count, width), BF16)] * 2,
        compiler_params=params(24),
        cost_estimate=cost(60 * rows * count * width, 6 * rows * width),
        name="combine",
    )(routes_t, gates_t, home)
    kept = half // groups
    other = pl.pallas_call(
        other_kernel,
        in_specs=[smem, vmem],
        out_shape=jax.ShapeDtypeStruct((kept, early_sum.shape[1]), BF16),
        compiler_params=params(8),
        cost_estimate=cost(60 * rows * count * width, 4 * kept * width),
        name="other",
    )(which, early_sum)
    came_early = lax.ppermute(other, "expert", route)
    grad_weights = pl.pallas_call(
        functools.partial(join_kernel, early_cols, late_cols),
        in_specs=[smem, vmem, vmem, vmem],
        out_shape=jax.ShapeDtypeStruct((1, kept, 3 * ff), BF16),
        compiler_params=params(8),
        name="join",
    )(which, early_sum, came_early, late_sum)
    return (layer_out, grad_tokens, grad_weights)


def solution(mesh):
    placed = (
        P(("dp", "expert"), None),
        P(("dp", "expert"), None),
        P(("dp", "expert"), None),
        P(("dp", "expert"), None),
        P("expert", None, None),
    )
    return jax.shard_map(
        local,
        mesh=mesh,
        in_specs=placed,
        out_specs=(P(("dp", "expert"), None), P(("dp", "expert"), None), P("expert", "dp", None)),
        check_vma=False,
    )
```

```python
import functools

import jax
import jax.numpy as jnp
from jax import lax
from jax.experimental import pallas as pl
from jax.experimental.pallas import tpu as pltpu
from jax.sharding import PartitionSpec as P

BF16 = jnp.bfloat16
F32 = jnp.float32
CAP = 14
ROWS = 16
LANES = 128


def dot(a, b, dims):
    return lax.dot_general(a, b, (dims, ((), ())), preferred_element_type=F32)


def dispatch_mask(routes, slots):
    top, tokens = routes.shape
    slot = lax.broadcasted_iota(jnp.int32, (slots, tokens), 0)
    names = [routes[k : k + 1, :] == slot for k in range(top)]
    named = names[0]
    for one in names[1:]:
        named = named | one
    earlier = (
        lax.broadcasted_iota(jnp.int32, (tokens, tokens), 0)
        < lax.broadcasted_iota(jnp.int32, (tokens, tokens), 1)
    )
    place = dot(
        jnp.where(named, 1.0, 0.0).astype(BF16),
        jnp.where(earlier, 1.0, 0.0).astype(BF16),
        ((1,), (0,)),
    ).astype(jnp.int32)
    return names, jnp.where(named, place, ROWS)


def by_slot(place):
    at = lax.broadcasted_iota(jnp.int32, (place.shape[0], ROWS, place.shape[1]), 1)
    return place[:, None, :] == at


def by_place(place):
    at = lax.broadcasted_iota(jnp.int32, (CAP,) + place.shape, 0)
    return place[None, :, :] == at


def onehot(mask):
    return jnp.where(mask, 1.0, 0.0).astype(BF16)


def strip_rows(slots, columns):
    row = lax.broadcasted_iota(jnp.int32, (slots * ROWS, columns), 0)
    col = lax.broadcasted_iota(jnp.int32, (slots * ROWS, columns), 1)
    return onehot(row == (col % slots) * ROWS + CAP + col // slots)


def strip_picks(slots):
    row = lax.broadcasted_iota(jnp.int32, (2 * slots, slots * ROWS), 0)
    col = lax.broadcasted_iota(jnp.int32, (2 * slots, slots * ROWS), 1)
    return onehot(col == (row % slots) * ROWS + CAP + row // slots)


def to_strips(tail, slots):
    strips = [
        jnp.concatenate(
            [
                tail[j * slots : (j + 1) * slots, q * LANES : (q + 1) * LANES]
                for j in range(CAP)
            ],
            axis=1,
        )
        for q in range(2)
    ]
    return jnp.concatenate(strips, axis=0)


def from_strips(strips, slots):
    tails = [
        jnp.concatenate(
            [
                strips[q * slots : (q + 1) * slots, j * LANES : (j + 1) * LANES]
                for j in range(CAP)
            ],
            axis=0,
        )
        for q in range(2)
    ]
    return jnp.concatenate(tails, axis=1)


def slot_gates(names, gates):
    total = jnp.where(names[0], gates[0:1, :], 0.0)
    for k in range(1, len(names)):
        total = total + jnp.where(names[k], gates[k : k + 1, :], 0.0)
    return total


def pack_kernel(
    routes_hbm,
    gates_hbm,
    tokens_hbm,
    out_grad_hbm,
    send_hbm,
    routes_ref,
    gates_ref,
    tokens_ref,
    out_grad_ref,
    send_ref,
    in_sems,
    out_sems,
):
    slots, _, main = send_ref.shape
    pieces = out_sems.shape[0]
    step = main // pieces
    pairs = (
        (routes_hbm, routes_ref),
        (gates_hbm, gates_ref),
        (tokens_hbm, tokens_ref),
        (out_grad_hbm, out_grad_ref),
    )
    loads = [pltpu.make_async_copy(*pair, in_sems.at[i]) for i, pair in enumerate(pairs)]
    for load in loads:
        load.start()
    loads[0].wait()
    names, place = dispatch_mask(routes_ref[...], slots)
    mask, turned = by_slot(place), by_place(place)
    rows = slots * ROWS
    pick = jnp.concatenate([onehot(mask).reshape(rows, -1), strip_rows(slots, LANES)], axis=1)
    tail_pick = onehot(turned).reshape(CAP * slots, -1)
    loads[1].wait()
    weight = slot_gates(names, gates_ref[...])
    row_gate = jnp.sum(jnp.where(mask, weight[:, None, :], 0.0), axis=2, keepdims=True)
    row_gate = jnp.where(
        lax.broadcasted_iota(jnp.int32, row_gate.shape, 1) < CAP, row_gate, 1.0
    )
    tail_gate = jnp.sum(jnp.where(turned, weight[None, :, :], 0.0), axis=2, keepdims=True)
    tail_gate = tail_gate.reshape(CAP * slots, 1)
    loads[2].wait()
    loads[3].wait()
    x_tail = dot(tail_pick, tokens_ref[:, main:], ((1,), (0,)))
    dy_tail = dot(tail_pick, out_grad_ref[:, main:], ((1,), (0,))) * tail_gate
    blank = jnp.zeros((LANES - 2 * slots, main), BF16)
    x_strips = jnp.concatenate([to_strips(x_tail.astype(BF16), slots), blank], axis=0)
    dy_strips = jnp.concatenate([to_strips(dy_tail.astype(BF16), slots), blank], axis=0)
    stores = []
    for piece in range(pieces):
        at = slice(piece * step, (piece + 1) * step)
        cols = pl.ds(piece * step, step)
        source = jnp.concatenate([tokens_ref[:, at], x_strips[:, at]], axis=0)
        x = dot(pick, source, ((1,), (0,)))
        send_ref[:, :ROWS, cols] = x.astype(BF16).reshape(slots, ROWS, step)
        source = jnp.concatenate([out_grad_ref[:, at], dy_strips[:, at]], axis=0)
        g = dot(pick, source, ((1,), (0,))).reshape(slots, ROWS, step)
        send_ref[:, ROWS:, cols] = (row_gate * g).astype(BF16)
        stores.append(
            pltpu.make_async_copy(
                send_ref.at[:, :, cols], send_hbm.at[:, :, cols], out_sems.at[piece]
            )
        )
        stores[-1].start()
    for store in stores:
        store.wait()


def unpack_rows(rows_ref, begin, out_ref):
    slots, _, main = rows_ref.shape
    rows = slots * ROWS
    came = rows_ref[:, begin : begin + ROWS, :]
    live = lax.broadcasted_iota(jnp.int32, (1, ROWS, 1), 1) < CAP
    out_ref[:, :main] = jnp.where(live, came, jnp.zeros((), BF16)).reshape(rows, main)
    strips = dot(strip_picks(slots), came.reshape(rows, main), ((1,), (0,))).astype(BF16)
    row = lax.broadcasted_iota(jnp.int32, (rows, CAP * slots), 0)
    col = lax.broadcasted_iota(jnp.int32, (rows, CAP * slots), 1)
    turn = onehot(col == (row % ROWS) * slots + row // ROWS)
    out_ref[:, main:] = dot(turn, from_strips(strips, slots), ((1,), (0,))).astype(BF16)


def expert_rows(x_ref, dy_ref, g, u, v, qg_ref, qu_ref, h_ref):
    x = x_ref[...]
    dy = dy_ref[...]
    a = dot(x, g, ((1,), (0,)))
    b = dot(x, u, ((1,), (0,)))
    e = dot(dy, v, ((1,), (0,)))
    s = jax.nn.sigmoid(a)
    active = a * s
    h_ref[...] = (active * b).astype(BF16)
    qg_ref[...] = (e * b * s * (1.0 + a * (1.0 - s))).astype(BF16)
    qu_ref[...] = (e * active).astype(BF16)


def early_kernel(
    plan,
    groups,
    rows_ref,
    w_ref,
    partial_ref,
    qg_ref,
    qu_ref,
    h_ref,
    x_hbm,
    dy_hbm,
    x_ref,
    dy_ref,
    sems,
):
    width = x_ref.shape[1]
    block = width // 2 // groups
    refs = (qg_ref, qu_ref, h_ref)

    def copies():
        return [
            pltpu.make_async_copy(x_ref, x_hbm, sems.at[0]),
            pltpu.make_async_copy(dy_ref, dy_hbm, sems.at[1]),
        ]

    for step, (j, n) in enumerate(plan):

        @pl.when(pl.program_id(0) == step)
        def _(step=step, j=j, n=n):
            if step == 0:
                unpack_rows(rows_ref, 0, x_ref)
                unpack_rows(rows_ref, ROWS, dy_ref)
                for copy in copies():
                    copy.start()
            if n is None:
                chunk, ff = h_ref.shape[1], w_ref.shape[1] // 3
                begins = [n * ff + j * chunk for n in range(3)]
                weights = (w_ref[:, at : at + chunk] for at in begins)
                expert_rows(x_ref, dy_ref, *weights, *refs)
                return
            lhs_ref = dy_ref if n == 2 else x_ref
            value = dot(lhs_ref[...], refs[n][...], ((0,), (0,))).astype(BF16)
            for half in range(2):
                for d in range(groups):
                    old, new = (half * groups + d) * block, (2 * d + half) * block
                    partial_ref[new : new + block] = value[old : old + block]
            if step == len(plan) - 1:
                for copy in copies():
                    copy.wait()


def late_kernel(
    plan,
    which_ref,
    x_ref,
    dy_ref,
    g_ref,
    u_ref,
    v_ref,
    kept_ref,
    own_ref,
    sent_ref,
    qg_ref,
    qu_ref,
    h_ref,
):
    half = x_ref.shape[1] // 2
    refs = (qg_ref, qu_ref, h_ref)
    for step, (j, n) in enumerate(plan):

        @pl.when(pl.program_id(0) == step)
        def _(j=j, n=n):
            if n is None:
                expert_rows(x_ref, dy_ref, g_ref[...], u_ref[...], v_ref[...], *refs)
                return
            rhs = refs[n][...] if j == 0 else kept_ref[...]
            lhs_ref = dy_ref if n == 2 else x_ref
            for out_ref, which in ((own_ref, which_ref[0]), (sent_ref, 1 - which_ref[0])):
                cols = pl.ds(pl.multiple_of(which * half, half), half)
                out_ref[...] = dot(lhs_ref[:, cols], rhs, ((0,), (0,))).astype(BF16)


def back_kernel(
    h0_ref, qg0_ref, qu0_ref, h_ref, qg_ref, qu_ref, w_ref, tail_ref, out_ref, strips_ref
):
    slots, _, block = out_ref.shape
    rows = slots * ROWS
    chunk = h0_ref.shape[1]
    ff = w_ref.shape[1] // 3
    at = pl.program_id(0)

    def product(first_ref, rest_ref, lines_ref, base):
        value = dot(first_ref[...], lines_ref[:, base : base + chunk], ((1,), (1,)))
        rest = lines_ref[:, base + chunk : base + ff]
        return value + dot(rest_ref[...], rest, ((1,), (1,)))

    def both(lines_ref):
        y = product(h0_ref, h_ref, lines_ref, 2 * ff)
        dx = product(qg0_ref, qg_ref, lines_ref, 0) + product(qu0_ref, qu_ref, lines_ref, ff)
        return y, dx

    @pl.when(at == 0)
    def _():
        row = lax.broadcasted_iota(jnp.int32, (CAP * slots, rows), 0)
        col = lax.broadcasted_iota(jnp.int32, (CAP * slots, rows), 1)
        turn = onehot(col == (row % slots) * ROWS + row // slots)
        for i, value in enumerate(both(tail_ref)):
            tail = dot(turn, value.astype(BF16), ((1,), (0,))).astype(BF16)
            strips = to_strips(tail, slots)
            for p in range(strips_ref.shape[0]):
                strips_ref[p, i] = strips[:, p * block : (p + 1) * block]

    spread = strip_rows(slots, 2 * slots)
    for i, value in enumerate(both(w_ref)):
        value = value.astype(BF16).astype(F32) + dot(spread, strips_ref[at, i], ((1,), (0,)))
        out_ref[:, i * ROWS : (i + 1) * ROWS, :] = value.astype(BF16).reshape(slots, ROWS, block)


def combine_kernel(routes_ref, gates_ref, back_ref, layer_ref, grad_ref):
    slots, _, main = back_ref.shape
    rows = slots * ROWS
    names, place = dispatch_mask(routes_ref[...], slots)
    weight = slot_gates(names, gates_ref[...])

    def split(mask, value):
        gate = jnp.where(mask, value, 0.0).reshape(-1, value.shape[-1])
        high = gate.astype(BF16)
        return high, (gate - high.astype(F32)).astype(BF16)

    mask, turned = by_slot(place), by_place(place)
    high, low = split(mask, weight[:, None, :])
    tail_high, tail_low = split(turned, weight[None, :, :])
    pick = onehot(mask).reshape(rows, -1)
    tail_pick = onehot(turned).reshape(CAP * slots, -1)
    take = strip_picks(slots)
    step = 256
    y_strips, dx_strips = [], []
    for c in range(0, main, step):
        cols = slice(c, c + step)
        y = back_ref[:, :ROWS, cols].reshape(rows, step)
        value = dot(high, y, ((0,), (0,))) + dot(low, y, ((0,), (0,)))
        layer_ref[:, cols] = value.astype(BF16)
        y_strips.append(dot(take, y, ((1,), (0,))).astype(BF16))
        dx = back_ref[:, ROWS:, cols].reshape(rows, step)
        grad_ref[:, cols] = dot(pick, dx, ((0,), (0,))).astype(BF16)
        dx_strips.append(dot(take, dx, ((1,), (0,))).astype(BF16))
    y = from_strips(jnp.concatenate(y_strips, axis=1), slots)
    value = dot(tail_high, y, ((0,), (0,))) + dot(tail_low, y, ((0,), (0,)))
    layer_ref[:, main:] = value.astype(BF16)
    dx = from_strips(jnp.concatenate(dx_strips, axis=1), slots)
    grad_ref[:, main:] = dot(tail_pick, dx, ((0,), (0,))).astype(BF16)


def other_kernel(which_ref, summed_ref, out_ref):
    half = out_ref.shape[0]
    begin = pl.multiple_of((1 - which_ref[0]) * half, half)
    out_ref[...] = summed_ref[pl.ds(begin, half), :]


def join_kernel(early_plan, late_plan, which_ref, early_ref, came_ref, late_ref, out_ref):
    half, columns = came_ref.shape
    chunk = columns // len(early_plan)
    steps = out_ref.shape[2] // 3 // chunk
    own = early_ref[pl.ds(pl.multiple_of(which_ref[0] * half, half), half), :]
    total = (own.astype(F32) + came_ref[...].astype(F32)).astype(BF16)
    for plan, value in ((early_plan, total), (late_plan, late_ref[...])):
        for i, (j, n) in enumerate(plan):
            new = (n * steps + j) * chunk
            out_ref[0, :, new : new + chunk] = value[:, i * chunk : (i + 1) * chunk]


def params(mib):
    return pltpu.CompilerParams(vmem_limit_bytes=int(mib * 1024 * 1024))


def cost(flops, moved):
    return pl.CostEstimate(flops=flops, bytes_accessed=moved, transcendentals=0)


def local(tokens, out_grad, routes, gates, weights):
    slots = lax.axis_size("expert")
    groups = lax.axis_size("dp")
    count, width = tokens.shape
    top = routes.shape[1]
    weight = weights[0]
    ff = weight.shape[1] // 3
    rows = slots * ROWS
    chunk = 256
    steps = ff // chunk
    half = width // 2
    routes_t = routes.T
    gates_t = gates.T
    upper = (lax.axis_index("expert") >= slots // 2).astype(jnp.int32)
    which = upper.reshape(1)
    smem = pl.BlockSpec(memory_space=pltpu.SMEM)
    vmem = pl.BlockSpec(memory_space=pltpu.VMEM)
    main = width - 2 * LANES
    pair = pltpu.HBM((slots, 2 * ROWS, main), BF16)
    flat = pltpu.HBM((rows, width), BF16)
    hbm = pl.BlockSpec(memory_space=pltpu.HBM)
    sent = pl.pallas_call(
        pack_kernel,
        in_specs=[hbm] * 4,
        out_specs=hbm,
        out_shape=pair,
        scratch_shapes=[
            pltpu.VMEM((top, count), jnp.int32),
            pltpu.VMEM((top, count), F32),
            pltpu.VMEM((count, width), BF16),
            pltpu.VMEM((count, width), BF16),
            pltpu.VMEM((slots, 2 * ROWS, main), BF16),
            pltpu.SemaphoreType.DMA((4,)),
            pltpu.SemaphoreType.DMA((7,)),
        ],
        compiler_params=params(54.2),
        cost_estimate=cost(4 * rows * count * width, 6 * rows * width),
        name="pack",
    )(routes_t, gates_t, tokens, out_grad)
    came = lax.all_to_all(sent, "expert", split_axis=0, concat_axis=0, tiled=True)

    early_plan = ((1, None), (1, 0), (1, 1), (2, None), (2, 0), (2, 1), (2, 2))
    late_plan = ((0, None), (0, 0), (0, 1), (0, 2), (1, 2))
    early_cols = tuple(one for one in early_plan if one[1] is not None)
    late_cols = tuple(one for one in late_plan if one[1] is not None)
    state = pltpu.HBM((rows, ff - chunk), BF16)
    state_spec = pl.BlockSpec((rows, chunk), lambda p: (0, jnp.where(p >= 3, 1, 0)))
    early, qg, qu, h, x, dy = pl.pallas_call(
        functools.partial(early_kernel, early_plan, groups),
        grid=(len(early_plan),),
        in_specs=[vmem, vmem],
        out_specs=[
            pl.BlockSpec(
                (width, chunk), lambda p: (0, p - jnp.where(p > 0, 1, 0) - jnp.where(p > 3, 1, 0))
            )
        ]
        + [state_spec] * 3
        + [hbm] * 2,
        out_shape=[pltpu.HBM((width, len(early_cols) * chunk), BF16)] + [state] * 3 + [flat] * 2,
        scratch_shapes=[
            pltpu.VMEM((rows, width), BF16),
            pltpu.VMEM((rows, width), BF16),
            pltpu.SemaphoreType.DMA((2,)),
        ],
        compiler_params=params(26),
        cost_estimate=cost(8 * rows * width * ff, 16 * width * ff),
        name="early_grads",
    )(came, weight)
    early_sum = lax.psum_scatter(early, "dp", scatter_dimension=0, tiled=True)
    state = pltpu.HBM((rows, chunk), BF16)
    state_spec = pl.BlockSpec((rows, chunk), lambda p: (0, 0))
    half_spec = pl.BlockSpec((half, chunk), lambda p: (0, jnp.maximum(p - 1, 0)))
    own, sent_half, qg0, qu0, h0 = pl.pallas_call(
        functools.partial(late_kernel, late_plan),
        grid=(len(late_plan),),
        in_specs=[smem]
        + [pl.BlockSpec((rows, width), lambda p: (0, 0))] * 2
        + [pl.BlockSpec((width, chunk), lambda p, n=n: (0, n * steps)) for n in range(3)]
        + [state_spec],
        out_specs=[half_spec] * 2 + [state_spec] * 3,
        out_shape=[pltpu.HBM((half, len(late_cols) * chunk), BF16)] * 2 + [state] * 3,
        compiler_params=params(63),
        cost_estimate=cost(4 * rows * width * ff, 8 * width * ff),
        name="late_grads",
    )(which, x, dy, weight, weight, weight, h)
    route = [((i + slots // 2) % slots, i) for i in range(slots)]
    came_half = lax.ppermute(sent_half, "expert", route)
    block = main // 2
    back = pl.pallas_call(
        back_kernel,
        grid=(main // block,),
        in_specs=[pl.BlockSpec((rows, chunk), lambda j: (0, 0))] * 3
        + [pl.BlockSpec((rows, ff - chunk), lambda j: (0, 0))] * 3
        + [
            pl.BlockSpec((block, 3 * ff), lambda j: (j, 0)),
            pl.BlockSpec((2 * LANES, 3 * ff), lambda j: (main // (2 * LANES), 0)),
        ],
        out_specs=pl.BlockSpec((slots, 2 * ROWS, block), lambda j: (0, 0, j)),
        out_shape=pair,
        scratch_shapes=[pltpu.VMEM((main // block, 2, 2 * slots, block), BF16)],
        compiler_params=params(63),
        cost_estimate=cost(6 * rows * width * ff, 12 * width * ff),
        name="back",
    )(h0, qg0, qu0, h, qg, qu, weight, weight)
    home = lax.all_to_all(back, "expert", split_axis=0, concat_axis=0, tiled=True)
    late = (own.astype(F32) + came_half.astype(F32)).astype(BF16)
    late_sum = lax.psum_scatter(late, "dp", scatter_dimension=0, tiled=True)
    layer_out, grad_tokens = pl.pallas_call(
        combine_kernel,
        out_shape=[jax.ShapeDtypeStruct((count, width), BF16)] * 2,
        compiler_params=params(24),
        cost_estimate=cost(60 * rows * count * width, 6 * rows * width),
        name="combine",
    )(routes_t, gates_t, home)
    kept = half // groups
    other = pl.pallas_call(
        other_kernel,
        in_specs=[smem, vmem],
        out_shape=jax.ShapeDtypeStruct((kept, early_sum.shape[1]), BF16),
        compiler_params=params(8),
        cost_estimate=cost(60 * rows * count * width, 4 * kept * width),
        name="other",
    )(which, early_sum)
    came_early = lax.ppermute(other, "expert", route)
    grad_weights = pl.pallas_call(
        functools.partial(join_kernel, early_cols, late_cols),
        in_specs=[smem, vmem, vmem, vmem],
        out_shape=jax.ShapeDtypeStruct((1, kept, 3 * ff), BF16),
        compiler_params=params(8),
        name="join",
    )(which, early_sum, came_early, late_sum)
    return (layer_out, grad_tokens, grad_weights)


def solution(mesh):
    placed = (
        P(("dp", "expert"), None),
        P(("dp", "expert"), None),
        P(("dp", "expert"), None),
        P(("dp", "expert"), None),
        P("expert", None, None),
    )
    return jax.shard_map(
        local,
        mesh=mesh,
        in_specs=placed,
        out_specs=(P(("dp", "expert"), None), P(("dp", "expert"), None), P("expert", "dp", None)),
        check_vma=False,
    )
```

```python
import functools

import jax
import jax.numpy as jnp
from jax import lax
from jax.experimental import pallas as pl
from jax.experimental.pallas import tpu as pltpu
from jax.sharding import PartitionSpec as P

BF16 = jnp.bfloat16
F32 = jnp.float32
CAP = 14
ROWS = 16
LANES = 128


def dot(a, b, dims):
    return lax.dot_general(a, b, (dims, ((), ())), preferred_element_type=F32)


def dispatch_mask(routes, slots):
    top, tokens = routes.shape
    slot = lax.broadcasted_iota(jnp.int32, (slots, tokens), 0)
    names = [routes[k : k + 1, :] == slot for k in range(top)]
    named = names[0]
    for one in names[1:]:
        named = named | one
    earlier = (
        lax.broadcasted_iota(jnp.int32, (tokens, tokens), 0)
        < lax.broadcasted_iota(jnp.int32, (tokens, tokens), 1)
    )
    place = dot(
        jnp.where(named, 1.0, 0.0).astype(BF16),
        jnp.where(earlier, 1.0, 0.0).astype(BF16),
        ((1,), (0,)),
    ).astype(jnp.int32)
    return names, jnp.where(named, place, ROWS)


def by_slot(place):
    at = lax.broadcasted_iota(jnp.int32, (place.shape[0], ROWS, place.shape[1]), 1)
    return place[:, None, :] == at


def by_place(place):
    at = lax.broadcasted_iota(jnp.int32, (CAP,) + place.shape, 0)
    return place[None, :, :] == at


def onehot(mask):
    return jnp.where(mask, 1.0, 0.0).astype(BF16)


def strip_rows(slots, columns):
    row = lax.broadcasted_iota(jnp.int32, (slots * ROWS, columns), 0)
    col = lax.broadcasted_iota(jnp.int32, (slots * ROWS, columns), 1)
    return onehot(row == (col % slots) * ROWS + CAP + col // slots)


def strip_picks(slots):
    row = lax.broadcasted_iota(jnp.int32, (2 * slots, slots * ROWS), 0)
    col = lax.broadcasted_iota(jnp.int32, (2 * slots, slots * ROWS), 1)
    return onehot(col == (row % slots) * ROWS + CAP + row // slots)


def to_strips(tail, slots):
    strips = [
        jnp.concatenate(
            [
                tail[j * slots : (j + 1) * slots, q * LANES : (q + 1) * LANES]
                for j in range(CAP)
            ],
            axis=1,
        )
        for q in range(2)
    ]
    return jnp.concatenate(strips, axis=0)


def from_strips(strips, slots):
    tails = [
        jnp.concatenate(
            [
                strips[q * slots : (q + 1) * slots, j * LANES : (j + 1) * LANES]
                for j in range(CAP)
            ],
            axis=0,
        )
        for q in range(2)
    ]
    return jnp.concatenate(tails, axis=1)


def slot_gates(names, gates):
    total = jnp.where(names[0], gates[0:1, :], 0.0)
    for k in range(1, len(names)):
        total = total + jnp.where(names[k], gates[k : k + 1, :], 0.0)
    return total


def pack_kernel(
    routes_hbm,
    gates_hbm,
    tokens_hbm,
    out_grad_hbm,
    send_hbm,
    routes_ref,
    gates_ref,
    tokens_ref,
    out_grad_ref,
    send_ref,
    in_sems,
    out_sems,
):
    slots, _, main = send_ref.shape
    pieces = out_sems.shape[0]
    step = main // pieces
    pairs = (
        (routes_hbm, routes_ref),
        (gates_hbm, gates_ref),
        (tokens_hbm, tokens_ref),
        (out_grad_hbm, out_grad_ref),
    )
    loads = [pltpu.make_async_copy(*pair, in_sems.at[i]) for i, pair in enumerate(pairs)]
    for load in loads:
        load.start()
    loads[0].wait()
    names, place = dispatch_mask(routes_ref[...], slots)
    mask, turned = by_slot(place), by_place(place)
    rows = slots * ROWS
    pick = jnp.concatenate([onehot(mask).reshape(rows, -1), strip_rows(slots, LANES)], axis=1)
    tail_pick = onehot(turned).reshape(CAP * slots, -1)
    loads[1].wait()
    weight = slot_gates(names, gates_ref[...])
    row_gate = jnp.sum(jnp.where(mask, weight[:, None, :], 0.0), axis=2, keepdims=True)
    row_gate = jnp.where(
        lax.broadcasted_iota(jnp.int32, row_gate.shape, 1) < CAP, row_gate, 1.0
    )
    tail_gate = jnp.sum(jnp.where(turned, weight[None, :, :], 0.0), axis=2, keepdims=True)
    tail_gate = tail_gate.reshape(CAP * slots, 1)
    loads[2].wait()
    loads[3].wait()
    x_tail = dot(tail_pick, tokens_ref[:, main:], ((1,), (0,)))
    dy_tail = dot(tail_pick, out_grad_ref[:, main:], ((1,), (0,))) * tail_gate
    blank = jnp.zeros((LANES - 2 * slots, main), BF16)
    x_strips = jnp.concatenate([to_strips(x_tail.astype(BF16), slots), blank], axis=0)
    dy_strips = jnp.concatenate([to_strips(dy_tail.astype(BF16), slots), blank], axis=0)
    stores = []
    for piece in range(pieces):
        at = slice(piece * step, (piece + 1) * step)
        cols = pl.ds(piece * step, step)
        source = jnp.concatenate([tokens_ref[:, at], x_strips[:, at]], axis=0)
        x = dot(pick, source, ((1,), (0,)))
        send_ref[:, :ROWS, cols] = x.astype(BF16).reshape(slots, ROWS, step)
        source = jnp.concatenate([out_grad_ref[:, at], dy_strips[:, at]], axis=0)
        g = dot(pick, source, ((1,), (0,))).reshape(slots, ROWS, step)
        send_ref[:, ROWS:, cols] = (row_gate * g).astype(BF16)
        stores.append(
            pltpu.make_async_copy(
                send_ref.at[:, :, cols], send_hbm.at[:, :, cols], out_sems.at[piece]
            )
        )
        stores[-1].start()
    for store in stores:
        store.wait()


def unpack_rows(rows_ref, begin, out_ref):
    slots, _, main = rows_ref.shape
    rows = slots * ROWS
    came = rows_ref[:, begin : begin + ROWS, :]
    live = lax.broadcasted_iota(jnp.int32, (1, ROWS, 1), 1) < CAP
    out_ref[:, :main] = jnp.where(live, came, jnp.zeros((), BF16)).reshape(rows, main)
    strips = dot(strip_picks(slots), came.reshape(rows, main), ((1,), (0,))).astype(BF16)
    row = lax.broadcasted_iota(jnp.int32, (rows, CAP * slots), 0)
    col = lax.broadcasted_iota(jnp.int32, (rows, CAP * slots), 1)
    turn = onehot(col == (row % ROWS) * slots + row // ROWS)
    out_ref[:, main:] = dot(turn, from_strips(strips, slots), ((1,), (0,))).astype(BF16)


def expert_rows(x_ref, dy_ref, g, u, v, qg_ref, qu_ref, h_ref):
    x = x_ref[...]
    dy = dy_ref[...]
    a = dot(x, g, ((1,), (0,)))
    b = dot(x, u, ((1,), (0,)))
    e = dot(dy, v, ((1,), (0,)))
    s = jax.nn.sigmoid(a)
    active = a * s
    h_ref[...] = (active * b).astype(BF16)
    qg_ref[...] = (e * b * s * (1.0 + a * (1.0 - s))).astype(BF16)
    qu_ref[...] = (e * active).astype(BF16)


def early_kernel(
    plan,
    groups,
    rows_ref,
    w_ref,
    partial_ref,
    qg_ref,
    qu_ref,
    h_ref,
    x_hbm,
    dy_hbm,
    x_ref,
    dy_ref,
    sems,
):
    width = x_ref.shape[1]
    block = width // 2 // groups
    refs = (qg_ref, qu_ref, h_ref)

    def copies():
        return [
            pltpu.make_async_copy(x_ref, x_hbm, sems.at[0]),
            pltpu.make_async_copy(dy_ref, dy_hbm, sems.at[1]),
        ]

    for step, (j, n) in enumerate(plan):

        @pl.when(pl.program_id(0) == step)
        def _(step=step, j=j, n=n):
            if step == 0:
                unpack_rows(rows_ref, 0, x_ref)
                unpack_rows(rows_ref, ROWS, dy_ref)
                for copy in copies():
                    copy.start()
            if n is None:
                chunk, ff = h_ref.shape[1], w_ref.shape[1] // 3
                begins = [n * ff + j * chunk for n in range(3)]
                weights = (w_ref[:, at : at + chunk] for at in begins)
                expert_rows(x_ref, dy_ref, *weights, *refs)
                return
            lhs_ref = dy_ref if n == 2 else x_ref
            value = dot(lhs_ref[...], refs[n][...], ((0,), (0,))).astype(BF16)
            for half in range(2):
                for d in range(groups):
                    old, new = (half * groups + d) * block, (2 * d + half) * block
                    partial_ref[new : new + block] = value[old : old + block]
            if step == len(plan) - 1:
                for copy in copies():
                    copy.wait()


def half_grads(x_ref, dy_ref, n, which, rhs):
    lhs_ref = dy_ref if n == 2 else x_ref
    half = lhs_ref.shape[1] // 2
    cols = pl.ds(pl.multiple_of(which * half, half), half)
    return dot(lhs_ref[:, cols], rhs, ((0,), (0,))).astype(BF16)


def late_kernel(
    plan, which_ref, x_ref, dy_ref, g_ref, u_ref, v_ref, sent_ref, qg_ref, qu_ref, h_ref
):
    refs = (qg_ref, qu_ref, h_ref)
    for step, n in enumerate(plan):

        @pl.when(pl.program_id(0) == step)
        def _(n=n):
            if n is None:
                expert_rows(x_ref, dy_ref, g_ref[...], u_ref[...], v_ref[...], *refs)
                return
            sent_ref[...] = half_grads(x_ref, dy_ref, n, 1 - which_ref[0], refs[n][...])


def later_kernel(
    plan, which_ref, x_ref, dy_ref, qg_ref, qu_ref, h_ref, kept_ref, sent_ref, own_ref
):
    refs = (qg_ref, qu_ref, h_ref)
    for step, (j, n, out) in enumerate(plan):

        @pl.when(pl.program_id(0) == step)
        def _(j=j, n=n, out=out):
            rhs = refs[n][...] if j == 0 else kept_ref[...]
            which = which_ref[0] if out else 1 - which_ref[0]
            (sent_ref, own_ref)[out][...] = half_grads(x_ref, dy_ref, n, which, rhs)


def late_sum_kernel(own_ref, came_ref, out_ref):
    out_ref[...] = (own_ref[...].astype(F32) + came_ref[...].astype(F32)).astype(BF16)


def late_join_kernel(first_ref, own_ref, came_ref, out_ref):
    columns = came_ref.shape[1]
    out_ref[:, :columns] = first_ref[...]
    total = own_ref[...].astype(F32) + came_ref[...].astype(F32)
    out_ref[:, columns:] = total.astype(BF16)


def back_kernel(
    h0_ref, qg0_ref, qu0_ref, h_ref, qg_ref, qu_ref, w_ref, tail_ref, out_ref, strips_ref
):
    slots, _, block = out_ref.shape
    rows = slots * ROWS
    chunk = h0_ref.shape[1]
    ff = w_ref.shape[1] // 3
    at = pl.program_id(0)

    def product(first_ref, rest_ref, lines_ref, base):
        value = dot(first_ref[...], lines_ref[:, base : base + chunk], ((1,), (1,)))
        rest = lines_ref[:, base + chunk : base + ff]
        return value + dot(rest_ref[...], rest, ((1,), (1,)))

    def both(lines_ref):
        y = product(h0_ref, h_ref, lines_ref, 2 * ff)
        dx = product(qg0_ref, qg_ref, lines_ref, 0) + product(qu0_ref, qu_ref, lines_ref, ff)
        return y, dx

    @pl.when(at == 0)
    def _():
        row = lax.broadcasted_iota(jnp.int32, (CAP * slots, rows), 0)
        col = lax.broadcasted_iota(jnp.int32, (CAP * slots, rows), 1)
        turn = onehot(col == (row % slots) * ROWS + row // slots)
        for i, value in enumerate(both(tail_ref)):
            tail = dot(turn, value.astype(BF16), ((1,), (0,))).astype(BF16)
            strips = to_strips(tail, slots)
            for p in range(strips_ref.shape[0]):
                strips_ref[p, i] = strips[:, p * block : (p + 1) * block]

    spread = strip_rows(slots, 2 * slots)
    for i, value in enumerate(both(w_ref)):
        value = value.astype(BF16).astype(F32) + dot(spread, strips_ref[at, i], ((1,), (0,)))
        out_ref[:, i * ROWS : (i + 1) * ROWS, :] = value.astype(BF16).reshape(slots, ROWS, block)


def combine_kernel(routes_ref, gates_ref, back_hbm, layer_ref, grad_ref, back_ref, sems):
    slots, _, main = back_ref.shape
    rows = slots * ROWS
    step = main // sems.shape[0]
    loads = []
    for c in range(0, main, step):
        cols = pl.ds(c, step)
        loads.append(
            pltpu.make_async_copy(
                back_hbm.at[:, :, cols], back_ref.at[:, :, cols], sems.at[c // step]
            )
        )
        loads[-1].start()
    names, place = dispatch_mask(routes_ref[...], slots)
    weight = slot_gates(names, gates_ref[...])

    def split(mask, value):
        gate = jnp.where(mask, value, 0.0).reshape(-1, value.shape[-1])
        high = gate.astype(BF16)
        return high, (gate - high.astype(F32)).astype(BF16)

    mask, turned = by_slot(place), by_place(place)
    high, low = split(mask, weight[:, None, :])
    tail_high, tail_low = split(turned, weight[None, :, :])
    pick = onehot(mask).reshape(rows, -1)
    tail_pick = onehot(turned).reshape(CAP * slots, -1)
    take = strip_picks(slots)
    y_strips, dx_strips = [], []
    for c in range(0, main, step):
        cols = slice(c, c + step)
        loads[c // step].wait()
        y = back_ref[:, :ROWS, cols].reshape(rows, step)
        value = dot(high, y, ((0,), (0,))) + dot(low, y, ((0,), (0,)))
        layer_ref[:, cols] = value.astype(BF16)
        y_strips.append(dot(take, y, ((1,), (0,))).astype(BF16))
        dx = back_ref[:, ROWS:, cols].reshape(rows, step)
        grad_ref[:, cols] = dot(pick, dx, ((0,), (0,))).astype(BF16)
        dx_strips.append(dot(take, dx, ((1,), (0,))).astype(BF16))
    y = from_strips(jnp.concatenate(y_strips, axis=1), slots)
    value = dot(tail_high, y, ((0,), (0,))) + dot(tail_low, y, ((0,), (0,)))
    layer_ref[:, main:] = value.astype(BF16)
    dx = from_strips(jnp.concatenate(dx_strips, axis=1), slots)
    grad_ref[:, main:] = dot(tail_pick, dx, ((0,), (0,))).astype(BF16)


def other_kernel(which_ref, summed_ref, out_ref):
    half = out_ref.shape[0]
    begin = pl.multiple_of((1 - which_ref[0]) * half, half)
    out_ref[...] = summed_ref[pl.ds(begin, half), :]


def join_kernel(early_plan, late_plan, which_ref, early_ref, came_ref, late_ref, out_ref):
    half, columns = came_ref.shape
    chunk = columns // len(early_plan)
    steps = out_ref.shape[2] // 3 // chunk
    own = early_ref[pl.ds(pl.multiple_of(which_ref[0] * half, half), half), :]
    total = (own.astype(F32) + came_ref[...].astype(F32)).astype(BF16)
    for plan, value in ((early_plan, total), (late_plan, late_ref[...])):
        for i, (j, n) in enumerate(plan):
            new = (n * steps + j) * chunk
            out_ref[0, :, new : new + chunk] = value[:, i * chunk : (i + 1) * chunk]


def params(mib):
    return pltpu.CompilerParams(vmem_limit_bytes=int(mib * 1024 * 1024))


def cost(flops, moved):
    return pl.CostEstimate(flops=flops, bytes_accessed=moved, transcendentals=0)


def local(tokens, out_grad, routes, gates, weights):
    slots = lax.axis_size("expert")
    groups = lax.axis_size("dp")
    count, width = tokens.shape
    top = routes.shape[1]
    weight = weights[0]
    ff = weight.shape[1] // 3
    rows = slots * ROWS
    chunk = 256
    steps = ff // chunk
    half = width // 2
    routes_t = routes.T
    gates_t = gates.T
    upper = (lax.axis_index("expert") >= slots // 2).astype(jnp.int32)
    which = upper.reshape(1)
    smem = pl.BlockSpec(memory_space=pltpu.SMEM)
    vmem = pl.BlockSpec(memory_space=pltpu.VMEM)
    main = width - 2 * LANES
    pair = pltpu.HBM((slots, 2 * ROWS, main), BF16)
    flat = pltpu.HBM((rows, width), BF16)
    hbm = pl.BlockSpec(memory_space=pltpu.HBM)
    sent = pl.pallas_call(
        pack_kernel,
        in_specs=[hbm] * 4,
        out_specs=hbm,
        out_shape=pair,
        scratch_shapes=[
            pltpu.VMEM((top, count), jnp.int32),
            pltpu.VMEM((top, count), F32),
            pltpu.VMEM((count, width), BF16),
            pltpu.VMEM((count, width), BF16),
            pltpu.VMEM((slots, 2 * ROWS, main), BF16),
            pltpu.SemaphoreType.DMA((4,)),
            pltpu.SemaphoreType.DMA((7,)),
        ],
        compiler_params=params(54.2),
        cost_estimate=cost(4 * rows * count * width, 6 * rows * width),
        name="pack",
    )(routes_t, gates_t, tokens, out_grad)
    came = lax.all_to_all(sent, "expert", split_axis=0, concat_axis=0, tiled=True)

    early_plan = ((1, None), (1, 0), (1, 1), (2, None), (2, 0), (2, 1), (2, 2))
    early_cols = tuple(one for one in early_plan if one[1] is not None)
    late_cols = ((0, 0), (0, 1), (0, 2), (1, 2))
    state = pltpu.HBM((rows, ff - chunk), BF16)
    state_spec = pl.BlockSpec((rows, chunk), lambda p: (0, jnp.where(p >= 3, 1, 0)))
    early, qg, qu, h, x, dy = pl.pallas_call(
        functools.partial(early_kernel, early_plan, groups),
        grid=(len(early_plan),),
        in_specs=[vmem, vmem],
        out_specs=[
            pl.BlockSpec(
                (width, chunk), lambda p: (0, p - jnp.where(p > 0, 1, 0) - jnp.where(p > 3, 1, 0))
            )
        ]
        + [state_spec] * 3
        + [hbm] * 2,
        out_shape=[pltpu.HBM((width, len(early_cols) * chunk), BF16)] + [state] * 3 + [flat] * 2,
        scratch_shapes=[
            pltpu.VMEM((rows, width), BF16),
            pltpu.VMEM((rows, width), BF16),
            pltpu.SemaphoreType.DMA((2,)),
        ],
        compiler_params=params(26),
        cost_estimate=cost(8 * rows * width * ff, 16 * width * ff),
        name="early_grads",
    )(came, weight)
    early_sum = lax.psum_scatter(early, "dp", scatter_dimension=0, tiled=True)
    state = pltpu.HBM((rows, chunk), BF16)
    state_spec = pl.BlockSpec((rows, chunk), lambda p: (0, 0))
    flat_spec = pl.BlockSpec((rows, width), lambda p: (0, 0))
    sent_shape = pltpu.HBM((half, 2 * chunk), BF16)
    sent_first, qg0, qu0, h0 = pl.pallas_call(
        functools.partial(late_kernel, (None, 0, 1)),
        grid=(3,),
        in_specs=[smem, flat_spec, flat_spec]
        + [pl.BlockSpec((width, chunk), lambda p, n=n: (0, n * steps)) for n in range(3)],
        out_specs=[pl.BlockSpec((half, chunk), lambda p: (0, jnp.maximum(p - 1, 0)))]
        + [state_spec] * 3,
        out_shape=[sent_shape] + [state] * 3,
        compiler_params=params(63),
        cost_estimate=cost(3 * rows * width * ff, 8 * width * ff),
        name="late_grads",
    )(which, x, dy, weight, weight, weight)
    route = [((i + slots // 2) % slots, i) for i in range(slots)]
    came_first = lax.ppermute(sent_first, "expert", route)
    plan = ((0, 2, 0), (1, 2, 0), (0, 0, 1), (0, 1, 1), (0, 2, 1), (1, 2, 1))
    sent_second, own = pl.pallas_call(
        functools.partial(later_kernel, plan),
        grid=(len(plan),),
        in_specs=[smem, flat_spec, flat_spec] + [state_spec] * 4,
        out_specs=[
            pl.BlockSpec((half, chunk), lambda p: (0, jnp.minimum(p, 1))),
            pl.BlockSpec((half, chunk), lambda p: (0, jnp.maximum(p - 2, 0))),
        ],
        out_shape=[sent_shape, pltpu.HBM((half, len(late_cols) * chunk), BF16)],
        compiler_params=params(63),
        cost_estimate=cost(2 * rows * width * ff, 8 * width * ff),
        name="later_grads",
    )(which, x, dy, qg0, qu0, h0, h)
    came_second = lax.ppermute(sent_second, "expert", route)
    block = main // 2
    back = pl.pallas_call(
        back_kernel,
        grid=(main // block,),
        in_specs=[pl.BlockSpec((rows, chunk), lambda j: (0, 0))] * 3
        + [pl.BlockSpec((rows, ff - chunk), lambda j: (0, 0))] * 3
        + [
            pl.BlockSpec((block, 3 * ff), lambda j: (j, 0)),
            pl.BlockSpec((2 * LANES, 3 * ff), lambda j: (main // (2 * LANES), 0)),
        ],
        out_specs=pl.BlockSpec((slots, 2 * ROWS, block), lambda j: (0, 0, j)),
        out_shape=pair,
        scratch_shapes=[pltpu.VMEM((main // block, 2, 2 * slots, block), BF16)],
        compiler_params=params(63),
        cost_estimate=cost(6 * rows * width * ff, 12 * width * ff),
        name="back",
    )(h0, qg0, qu0, h, qg, qu, weight, weight)
    home = lax.all_to_all(back, "expert", split_axis=0, concat_axis=0, tiled=True)
    lines = half // 4
    part_spec = pl.BlockSpec((lines, 2 * chunk), lambda p: (p, 0))
    late_first = pl.pallas_call(
        late_sum_kernel,
        grid=(4,),
        in_specs=[part_spec] * 2,
        out_specs=part_spec,
        out_shape=sent_shape,
        compiler_params=params(63),
        cost_estimate=cost(60 * rows * count * width, 16 * half * chunk),
        name="late_sum",
    )(own, came_first)
    late = pl.pallas_call(
        late_join_kernel,
        grid=(4,),
        in_specs=[part_spec, pl.BlockSpec((lines, 2 * chunk), lambda p: (p, 1)), part_spec],
        out_specs=pl.BlockSpec((lines, 4 * chunk), lambda p: (p, 0)),
        out_shape=pltpu.HBM((half, 4 * chunk), BF16),
        compiler_params=params(63),
        cost_estimate=cost(half * 4 * chunk, 24 * half * chunk),
        name="late_join",
    )(late_first, own, came_second)
    late_sum = lax.psum_scatter(late, "dp", scatter_dimension=0, tiled=True)
    layer_out, grad_tokens = pl.pallas_call(
        combine_kernel,
        in_specs=[vmem, vmem, hbm],
        scratch_shapes=[
            pltpu.VMEM((slots, 2 * ROWS, main), BF16),
            pltpu.SemaphoreType.DMA((7,)),
        ],
        out_shape=[jax.ShapeDtypeStruct((count, width), BF16)] * 2,
        compiler_params=params(63),
        cost_estimate=cost(60 * rows * count * width, 6 * rows * width),
        name="combine",
    )(routes_t, gates_t, home)
    kept = half // groups
    other = pl.pallas_call(
        other_kernel,
        in_specs=[smem, vmem],
        out_shape=jax.ShapeDtypeStruct((kept, early_sum.shape[1]), BF16),
        compiler_params=params(8),
        cost_estimate=cost(60 * rows * count * width, 4 * kept * width),
        name="other",
    )(which, early_sum)
    came_early = lax.ppermute(other, "expert", route)
    grad_weights = pl.pallas_call(
        functools.partial(join_kernel, early_cols, late_cols),
        in_specs=[smem, vmem, vmem, vmem],
        out_shape=jax.ShapeDtypeStruct((1, kept, 3 * ff), BF16),
        compiler_params=params(8),
        name="join",
    )(which, early_sum, came_early, late_sum)
    return (layer_out, grad_tokens, grad_weights)


def solution(mesh):
    placed = (
        P(("dp", "expert"), None),
        P(("dp", "expert"), None),
        P(("dp", "expert"), None),
        P(("dp", "expert"), None),
        P("expert", None, None),
    )
    return jax.shard_map(
        local,
        mesh=mesh,
        in_specs=placed,
        out_specs=(P(("dp", "expert"), None), P(("dp", "expert"), None), P("expert", "dp", None)),
        check_vma=False,
    )
```

```python
import functools

import jax
import jax.numpy as jnp
from jax import lax
from jax.experimental import pallas as pl
from jax.experimental.pallas import tpu as pltpu
from jax.sharding import PartitionSpec as P

BF16 = jnp.bfloat16
F32 = jnp.float32
CAP = 14
ROWS = 16
LANES = 128


def dot(a, b, dims):
    return lax.dot_general(a, b, (dims, ((), ())), preferred_element_type=F32)


def dispatch_mask(routes, slots):
    top, tokens = routes.shape
    slot = lax.broadcasted_iota(jnp.int32, (slots, tokens), 0)
    names = [routes[k : k + 1, :] == slot for k in range(top)]
    named = names[0]
    for one in names[1:]:
        named = named | one
    earlier = (
        lax.broadcasted_iota(jnp.int32, (tokens, tokens), 0)
        < lax.broadcasted_iota(jnp.int32, (tokens, tokens), 1)
    )
    place = dot(
        jnp.where(named, 1.0, 0.0).astype(BF16),
        jnp.where(earlier, 1.0, 0.0).astype(BF16),
        ((1,), (0,)),
    ).astype(jnp.int32)
    return names, jnp.where(named, place, ROWS)


def by_slot(place):
    at = lax.broadcasted_iota(jnp.int32, (place.shape[0], ROWS, place.shape[1]), 1)
    return place[:, None, :] == at


def by_place(place):
    at = lax.broadcasted_iota(jnp.int32, (CAP,) + place.shape, 0)
    return place[None, :, :] == at


def onehot(mask):
    return jnp.where(mask, 1.0, 0.0).astype(BF16)


def strip_rows(slots, columns):
    row = lax.broadcasted_iota(jnp.int32, (slots * ROWS, columns), 0)
    col = lax.broadcasted_iota(jnp.int32, (slots * ROWS, columns), 1)
    return onehot(row == (col % slots) * ROWS + CAP + col // slots)


def strip_picks(slots):
    row = lax.broadcasted_iota(jnp.int32, (2 * slots, slots * ROWS), 0)
    col = lax.broadcasted_iota(jnp.int32, (2 * slots, slots * ROWS), 1)
    return onehot(col == (row % slots) * ROWS + CAP + row // slots)


def to_strips(tail, slots):
    strips = [
        jnp.concatenate(
            [
                tail[j * slots : (j + 1) * slots, q * LANES : (q + 1) * LANES]
                for j in range(CAP)
            ],
            axis=1,
        )
        for q in range(2)
    ]
    return jnp.concatenate(strips, axis=0)


def from_strips(strips, slots):
    tails = [
        jnp.concatenate(
            [
                strips[q * slots : (q + 1) * slots, j * LANES : (j + 1) * LANES]
                for j in range(CAP)
            ],
            axis=0,
        )
        for q in range(2)
    ]
    return jnp.concatenate(tails, axis=1)


def slot_gates(names, gates):
    total = jnp.where(names[0], gates[0:1, :], 0.0)
    for k in range(1, len(names)):
        total = total + jnp.where(names[k], gates[k : k + 1, :], 0.0)
    return total


def pack_kernel(
    routes_hbm,
    gates_hbm,
    tokens_hbm,
    out_grad_hbm,
    send_hbm,
    routes_ref,
    gates_ref,
    tokens_ref,
    out_grad_ref,
    send_ref,
    in_sems,
    out_sems,
):
    slots, _, main = send_ref.shape
    pieces = out_sems.shape[0]
    step = main // pieces
    pairs = (
        (routes_hbm, routes_ref),
        (gates_hbm, gates_ref),
        (tokens_hbm, tokens_ref),
        (out_grad_hbm, out_grad_ref),
    )
    loads = [pltpu.make_async_copy(*pair, in_sems.at[i]) for i, pair in enumerate(pairs)]
    for load in loads:
        load.start()
    loads[0].wait()
    names, place = dispatch_mask(routes_ref[...], slots)
    mask, turned = by_slot(place), by_place(place)
    rows = slots * ROWS
    pick = jnp.concatenate([onehot(mask).reshape(rows, -1), strip_rows(slots, LANES)], axis=1)
    tail_pick = onehot(turned).reshape(CAP * slots, -1)
    loads[1].wait()
    weight = slot_gates(names, gates_ref[...])
    row_gate = jnp.sum(jnp.where(mask, weight[:, None, :], 0.0), axis=2, keepdims=True)
    row_gate = jnp.where(
        lax.broadcasted_iota(jnp.int32, row_gate.shape, 1) < CAP, row_gate, 1.0
    )
    tail_gate = jnp.sum(jnp.where(turned, weight[None, :, :], 0.0), axis=2, keepdims=True)
    tail_gate = tail_gate.reshape(CAP * slots, 1)
    loads[2].wait()
    loads[3].wait()
    x_tail = dot(tail_pick, tokens_ref[:, main:], ((1,), (0,)))
    dy_tail = dot(tail_pick, out_grad_ref[:, main:], ((1,), (0,))) * tail_gate
    blank = jnp.zeros((LANES - 2 * slots, main), BF16)
    x_strips = jnp.concatenate([to_strips(x_tail.astype(BF16), slots), blank], axis=0)
    dy_strips = jnp.concatenate([to_strips(dy_tail.astype(BF16), slots), blank], axis=0)
    stores = []
    for piece in range(pieces):
        at = slice(piece * step, (piece + 1) * step)
        cols = pl.ds(piece * step, step)
        source = jnp.concatenate([tokens_ref[:, at], x_strips[:, at]], axis=0)
        x = dot(pick, source, ((1,), (0,)))
        send_ref[:, :ROWS, cols] = x.astype(BF16).reshape(slots, ROWS, step)
        source = jnp.concatenate([out_grad_ref[:, at], dy_strips[:, at]], axis=0)
        g = dot(pick, source, ((1,), (0,))).reshape(slots, ROWS, step)
        send_ref[:, ROWS:, cols] = (row_gate * g).astype(BF16)
        stores.append(
            pltpu.make_async_copy(
                send_ref.at[:, :, cols], send_hbm.at[:, :, cols], out_sems.at[piece]
            )
        )
        stores[-1].start()
    for store in stores:
        store.wait()


def unpack_rows(rows_ref, begin, out_ref):
    slots, _, main = rows_ref.shape
    rows = slots * ROWS
    came = rows_ref[:, begin : begin + ROWS, :]
    live = lax.broadcasted_iota(jnp.int32, (1, ROWS, 1), 1) < CAP
    out_ref[:, :main] = jnp.where(live, came, jnp.zeros((), BF16)).reshape(rows, main)
    strips = dot(strip_picks(slots), came.reshape(rows, main), ((1,), (0,))).astype(BF16)
    row = lax.broadcasted_iota(jnp.int32, (rows, CAP * slots), 0)
    col = lax.broadcasted_iota(jnp.int32, (rows, CAP * slots), 1)
    turn = onehot(col == (row % ROWS) * slots + row // ROWS)
    out_ref[:, main:] = dot(turn, from_strips(strips, slots), ((1,), (0,))).astype(BF16)


def state_rows(a, b, e, qg_ref, qu_ref, h_ref):
    s = jax.nn.sigmoid(a)
    active = a * s
    h_ref[...] = (active * b).astype(BF16)
    qg_ref[...] = (e * b * s * (1.0 + a * (1.0 - s))).astype(BF16)
    qu_ref[...] = (e * active).astype(BF16)


def expert_rows(x_ref, dy_ref, g, u, v, qg_ref, qu_ref, h_ref):
    x = x_ref[...]
    a = dot(x, g, ((1,), (0,)))
    b = dot(x, u, ((1,), (0,)))
    e = dot(dy_ref[...], v, ((1,), (0,)))
    state_rows(a, b, e, qg_ref, qu_ref, h_ref)


def early_kernel(
    plan,
    groups,
    rows_ref,
    w_ref,
    partial_ref,
    qg_ref,
    qu_ref,
    h_ref,
    x_hbm,
    dy_hbm,
    x_ref,
    dy_ref,
    sems,
):
    width = x_ref.shape[1]
    block = width // 2 // groups
    refs = (qg_ref, qu_ref, h_ref)

    def copies():
        return [
            pltpu.make_async_copy(x_ref, x_hbm, sems.at[0]),
            pltpu.make_async_copy(dy_ref, dy_hbm, sems.at[1]),
        ]

    for step, (j, n) in enumerate(plan):

        @pl.when(pl.program_id(0) == step)
        def _(step=step, j=j, n=n):
            if step == 0:
                unpack_rows(rows_ref, 0, x_ref)
                unpack_rows(rows_ref, ROWS, dy_ref)
                for copy in copies():
                    copy.start()
            if n is None:
                chunk, ff = h_ref.shape[1], w_ref.shape[1] // 3
                begins = [n * ff + j * chunk for n in range(3)]
                weights = (w_ref[:, at : at + chunk] for at in begins)
                expert_rows(x_ref, dy_ref, *weights, *refs)
                return
            lhs_ref = dy_ref if n == 2 else x_ref
            value = dot(lhs_ref[...], refs[n][...], ((0,), (0,))).astype(BF16)
            for half in range(2):
                for d in range(groups):
                    old, new = (half * groups + d) * block, (2 * d + half) * block
                    partial_ref[new : new + block] = value[old : old + block]
            if step == len(plan) - 1:
                for copy in copies():
                    copy.wait()


def half_grads(x_ref, dy_ref, n, which, rhs):
    lhs_ref = dy_ref if n == 2 else x_ref
    half = lhs_ref.shape[1] // 2
    cols = pl.ds(pl.multiple_of(which * half, half), half)
    return dot(lhs_ref[:, cols], rhs, ((0,), (0,))).astype(BF16)


def late_kernel(
    plan,
    which_ref,
    x_hbm,
    dy_hbm,
    w_hbm,
    sent_ref,
    qg_ref,
    qu_ref,
    h_ref,
    x_ref,
    dy_ref,
    w_ref,
    sems,
):
    refs = (qg_ref, qu_ref, h_ref)
    chunk = h_ref.shape[1]
    ff = w_hbm.shape[1] // 3

    @pl.when(pl.program_id(0) == 0)
    def _():
        pairs = [(w_hbm.at[:, pl.ds(n * ff, chunk)], w_ref.at[n]) for n in range(3)]
        pairs = [(x_hbm, x_ref), pairs[0], pairs[1], (dy_hbm, dy_ref), pairs[2]]
        loads = [pltpu.make_async_copy(*pair, sems.at[i]) for i, pair in enumerate(pairs)]
        for load in loads:
            load.start()
        loads[0].wait()
        loads[1].wait()
        a = dot(x_ref[...], w_ref[0], ((1,), (0,)))
        loads[2].wait()
        b = dot(x_ref[...], w_ref[1], ((1,), (0,)))
        loads[3].wait()
        loads[4].wait()
        e = dot(dy_ref[...], w_ref[2], ((1,), (0,)))
        state_rows(a, b, e, *refs)

    for step, n in enumerate(plan):

        @pl.when(pl.program_id(0) == step + 1)
        def _(n=n):
            sent_ref[...] = half_grads(x_ref, dy_ref, n, 1 - which_ref[0], refs[n][...])


def later_kernel(
    plan, which_ref, x_ref, dy_ref, qg_ref, qu_ref, h_ref, kept_ref, sent_ref, own_ref
):
    refs = (qg_ref, qu_ref, h_ref)
    for step, (j, n, out) in enumerate(plan):

        @pl.when(pl.program_id(0) == step)
        def _(j=j, n=n, out=out):
            rhs = refs[n][...] if j == 0 else kept_ref[...]
            which = which_ref[0] if out else 1 - which_ref[0]
            (sent_ref, own_ref)[out][...] = half_grads(x_ref, dy_ref, n, which, rhs)


def late_sum_kernel(own_ref, came_ref, out_ref):
    out_ref[...] = (own_ref[...].astype(F32) + came_ref[...].astype(F32)).astype(BF16)


def late_join_kernel(first_ref, own_ref, came_ref, out_ref):
    columns = came_ref.shape[1]
    out_ref[:, :columns] = first_ref[...]
    total = own_ref[...].astype(F32) + came_ref[...].astype(F32)
    out_ref[:, columns:] = total.astype(BF16)


def back_kernel(
    h0_ref, qg0_ref, qu0_ref, h_ref, qg_ref, qu_ref, w_ref, tail_ref, out_ref, strips_ref
):
    slots, _, block = out_ref.shape
    rows = slots * ROWS
    chunk = h0_ref.shape[1]
    ff = w_ref.shape[1] // 3
    at = pl.program_id(0)

    def product(first_ref, rest_ref, lines_ref, base):
        value = dot(first_ref[...], lines_ref[:, base : base + chunk], ((1,), (1,)))
        rest = lines_ref[:, base + chunk : base + ff]
        return value + dot(rest_ref[...], rest, ((1,), (1,)))

    def both(lines_ref):
        y = product(h0_ref, h_ref, lines_ref, 2 * ff)
        dx = product(qg0_ref, qg_ref, lines_ref, 0) + product(qu0_ref, qu_ref, lines_ref, ff)
        return y, dx

    @pl.when(at == 0)
    def _():
        row = lax.broadcasted_iota(jnp.int32, (CAP * slots, rows), 0)
        col = lax.broadcasted_iota(jnp.int32, (CAP * slots, rows), 1)
        turn = onehot(col == (row % slots) * ROWS + row // slots)
        for i, value in enumerate(both(tail_ref)):
            tail = dot(turn, value.astype(BF16), ((1,), (0,))).astype(BF16)
            strips = to_strips(tail, slots)
            for p in range(strips_ref.shape[0]):
                strips_ref[p, i] = strips[:, p * block : (p + 1) * block]

    spread = strip_rows(slots, 2 * slots)
    for i, value in enumerate(both(w_ref)):
        value = value.astype(BF16).astype(F32) + dot(spread, strips_ref[at, i], ((1,), (0,)))
        out_ref[:, i * ROWS : (i + 1) * ROWS, :] = value.astype(BF16).reshape(slots, ROWS, block)


def combine_kernel(routes_ref, gates_ref, back_hbm, layer_ref, grad_ref, back_ref, sems):
    slots, _, main = back_ref.shape
    rows = slots * ROWS
    count = layer_ref.shape[0]
    step = main // sems.shape[0]
    loads = []
    for c in range(0, main, step):
        cols = pl.ds(c, step)
        loads.append(
            pltpu.make_async_copy(
                back_hbm.at[:, :, cols], back_ref.at[:, :, cols], sems.at[c // step]
            )
        )
        loads[-1].start()
    names, place = dispatch_mask(routes_ref[...], slots)
    weight = slot_gates(names, gates_ref[...])

    def split(gate):
        high = gate.astype(BF16)
        return [high, (gate - high.astype(F32)).astype(BF16)]

    def turned_rows(mask, value):
        return jnp.where(mask, value, 0.0).reshape(-1, value.shape[-1]).T

    mask, turned = by_slot(place), by_place(place)
    take = strip_picks(slots)
    y_pick = jnp.concatenate(split(turned_rows(mask, weight[:, None, :])) + [take], axis=0)
    dx_pick = turned_rows(mask, jnp.ones((1, 1, count), F32)).astype(BF16)
    dx_pick = jnp.concatenate([dx_pick, take], axis=0)
    y_strips, dx_strips = [], []
    for c in range(0, main, step):
        cols = slice(c, c + step)
        loads[c // step].wait()
        y = dot(y_pick, back_ref[:, :ROWS, cols].reshape(rows, step), ((1,), (0,)))
        layer_ref[:, cols] = (y[:count] + y[count : 2 * count]).astype(BF16)
        y_strips.append(y[2 * count :].astype(BF16))
        dx = dot(dx_pick, back_ref[:, ROWS:, cols].reshape(rows, step), ((1,), (0,)))
        grad_ref[:, cols] = dx[:count].astype(BF16)
        dx_strips.append(dx[count:].astype(BF16))
    high, low = split(turned_rows(turned, weight[None, :, :]))
    y = from_strips(jnp.concatenate(y_strips, axis=1), slots)
    value = dot(high, y, ((1,), (0,))) + dot(low, y, ((1,), (0,)))
    layer_ref[:, main:] = value.astype(BF16)
    pick = turned_rows(turned, jnp.ones((1, 1, count), F32)).astype(BF16)
    dx = from_strips(jnp.concatenate(dx_strips, axis=1), slots)
    grad_ref[:, main:] = dot(pick, dx, ((1,), (0,))).astype(BF16)


def other_kernel(which_ref, summed_ref, out_ref):
    half = out_ref.shape[0]
    begin = pl.multiple_of((1 - which_ref[0]) * half, half)
    out_ref[...] = summed_ref[pl.ds(begin, half), :]


def join_kernel(early_plan, late_plan, which_ref, early_ref, came_ref, late_ref, out_ref):
    half, columns = came_ref.shape
    chunk = columns // len(early_plan)
    steps = out_ref.shape[2] // 3 // chunk
    own = early_ref[pl.ds(pl.multiple_of(which_ref[0] * half, half), half), :]
    total = (own.astype(F32) + came_ref[...].astype(F32)).astype(BF16)
    for plan, value in ((early_plan, total), (late_plan, late_ref[...])):
        for i, (j, n) in enumerate(plan):
            new = (n * steps + j) * chunk
            out_ref[0, :, new : new + chunk] = value[:, i * chunk : (i + 1) * chunk]


def params(mib):
    return pltpu.CompilerParams(vmem_limit_bytes=int(mib * 1024 * 1024))


def cost(flops, moved):
    return pl.CostEstimate(flops=flops, bytes_accessed=moved, transcendentals=0)


def local(tokens, out_grad, routes, gates, weights):
    slots = lax.axis_size("expert")
    groups = lax.axis_size("dp")
    count, width = tokens.shape
    top = routes.shape[1]
    weight = weights[0]
    ff = weight.shape[1] // 3
    rows = slots * ROWS
    chunk = 256
    steps = ff // chunk
    half = width // 2
    routes_t = routes.T
    gates_t = gates.T
    upper = (lax.axis_index("expert") >= slots // 2).astype(jnp.int32)
    which = upper.reshape(1)
    smem = pl.BlockSpec(memory_space=pltpu.SMEM)
    vmem = pl.BlockSpec(memory_space=pltpu.VMEM)
    main = width - 2 * LANES
    pair = pltpu.HBM((slots, 2 * ROWS, main), BF16)
    flat = pltpu.HBM((rows, width), BF16)
    hbm = pl.BlockSpec(memory_space=pltpu.HBM)
    sent = pl.pallas_call(
        pack_kernel,
        in_specs=[hbm] * 4,
        out_specs=hbm,
        out_shape=pair,
        scratch_shapes=[
            pltpu.VMEM((top, count), jnp.int32),
            pltpu.VMEM((top, count), F32),
            pltpu.VMEM((count, width), BF16),
            pltpu.VMEM((count, width), BF16),
            pltpu.VMEM((slots, 2 * ROWS, main), BF16),
            pltpu.SemaphoreType.DMA((4,)),
            pltpu.SemaphoreType.DMA((7,)),
        ],
        compiler_params=params(54.2),
        cost_estimate=cost(4 * rows * count * width, 6 * rows * width),
        name="pack",
    )(routes_t, gates_t, tokens, out_grad)
    came = lax.all_to_all(sent, "expert", split_axis=0, concat_axis=0, tiled=True)

    early_plan = ((1, None), (1, 0), (1, 1), (2, None), (2, 0), (2, 1), (2, 2))
    early_cols = tuple(one for one in early_plan if one[1] is not None)
    late_cols = ((0, 0), (0, 1), (0, 2), (1, 2))
    state = pltpu.HBM((rows, ff - chunk), BF16)
    state_spec = pl.BlockSpec((rows, chunk), lambda p: (0, jnp.where(p >= 3, 1, 0)))
    early, qg, qu, h, x, dy = pl.pallas_call(
        functools.partial(early_kernel, early_plan, groups),
        grid=(len(early_plan),),
        in_specs=[vmem, vmem],
        out_specs=[
            pl.BlockSpec(
                (width, chunk), lambda p: (0, p - jnp.where(p > 0, 1, 0) - jnp.where(p > 3, 1, 0))
            )
        ]
        + [state_spec] * 3
        + [hbm] * 2,
        out_shape=[pltpu.HBM((width, len(early_cols) * chunk), BF16)] + [state] * 3 + [flat] * 2,
        scratch_shapes=[
            pltpu.VMEM((rows, width), BF16),
            pltpu.VMEM((rows, width), BF16),
            pltpu.SemaphoreType.DMA((2,)),
        ],
        compiler_params=params(26),
        cost_estimate=cost(8 * rows * width * ff, 16 * width * ff),
        name="early_grads",
    )(came, weight)
    early_sum = lax.psum_scatter(early, "dp", scatter_dimension=0, tiled=True)
    state = pltpu.HBM((rows, chunk), BF16)
    state_spec = pl.BlockSpec((rows, chunk), lambda p: (0, 0))
    flat_spec = pl.BlockSpec((rows, width), lambda p: (0, 0))
    sent_shape = pltpu.HBM((half, 2 * chunk), BF16)
    sent_first, qg0, qu0, h0 = pl.pallas_call(
        functools.partial(late_kernel, (0, 1)),
        grid=(3,),
        in_specs=[smem, hbm, hbm, hbm],
        out_specs=[pl.BlockSpec((half, chunk), lambda p: (0, jnp.maximum(p - 1, 0)))]
        + [state_spec] * 3,
        out_shape=[sent_shape] + [state] * 3,
        scratch_shapes=[
            pltpu.VMEM((rows, width), BF16),
            pltpu.VMEM((rows, width), BF16),
            pltpu.VMEM((3, width, chunk), BF16),
            pltpu.SemaphoreType.DMA((5,)),
        ],
        compiler_params=params(63),
        cost_estimate=cost(3 * rows * width * ff, 8 * width * ff),
        name="late_grads",
    )(which, x, dy, weight)
    route = [((i + slots // 2) % slots, i) for i in range(slots)]
    came_first = lax.ppermute(sent_first, "expert", route)
    plan = ((0, 2, 0), (1, 2, 0), (0, 0, 1), (0, 1, 1), (0, 2, 1), (1, 2, 1))
    sent_second, own = pl.pallas_call(
        functools.partial(later_kernel, plan),
        grid=(len(plan),),
        in_specs=[smem, flat_spec, flat_spec] + [state_spec] * 4,
        out_specs=[
            pl.BlockSpec((half, chunk), lambda p: (0, jnp.minimum(p, 1))),
            pl.BlockSpec((half, chunk), lambda p: (0, jnp.maximum(p - 2, 0))),
        ],
        out_shape=[sent_shape, pltpu.HBM((half, len(late_cols) * chunk), BF16)],
        compiler_params=params(63),
        cost_estimate=cost(2 * rows * width * ff, 8 * width * ff),
        name="later_grads",
    )(which, x, dy, qg0, qu0, h0, h)
    came_second = lax.ppermute(sent_second, "expert", route)
    block = main // 2
    back = pl.pallas_call(
        back_kernel,
        grid=(main // block,),
        in_specs=[pl.BlockSpec((rows, chunk), lambda j: (0, 0))] * 3
        + [pl.BlockSpec((rows, ff - chunk), lambda j: (0, 0))] * 3
        + [
            pl.BlockSpec((block, 3 * ff), lambda j: (j, 0)),
            pl.BlockSpec((2 * LANES, 3 * ff), lambda j: (main // (2 * LANES), 0)),
        ],
        out_specs=pl.BlockSpec((slots, 2 * ROWS, block), lambda j: (0, 0, j)),
        out_shape=pair,
        scratch_shapes=[pltpu.VMEM((main // block, 2, 2 * slots, block), BF16)],
        compiler_params=params(63),
        cost_estimate=cost(6 * rows * width * ff, 12 * width * ff),
        name="back",
    )(h0, qg0, qu0, h, qg, qu, weight, weight)
    home = lax.all_to_all(back, "expert", split_axis=0, concat_axis=0, tiled=True)
    lines = half // 4
    part_spec = pl.BlockSpec((lines, 2 * chunk), lambda p: (p, 0))
    late_first = pl.pallas_call(
        late_sum_kernel,
        grid=(4,),
        in_specs=[part_spec] * 2,
        out_specs=part_spec,
        out_shape=sent_shape,
        compiler_params=params(63),
        cost_estimate=cost(60 * rows * count * width, 16 * half * chunk),
        name="late_sum",
    )(own, came_first)
    late = pl.pallas_call(
        late_join_kernel,
        grid=(4,),
        in_specs=[part_spec, pl.BlockSpec((lines, 2 * chunk), lambda p: (p, 1)), part_spec],
        out_specs=pl.BlockSpec((lines, 4 * chunk), lambda p: (p, 0)),
        out_shape=pltpu.HBM((half, 4 * chunk), BF16),
        compiler_params=params(63),
        cost_estimate=cost(half * 4 * chunk, 24 * half * chunk),
        name="late_join",
    )(late_first, own, came_second)
    late_sum = lax.psum_scatter(late, "dp", scatter_dimension=0, tiled=True)
    layer_out, grad_tokens = pl.pallas_call(
        combine_kernel,
        in_specs=[vmem, vmem, hbm],
        scratch_shapes=[
            pltpu.VMEM((slots, 2 * ROWS, main), BF16),
            pltpu.SemaphoreType.DMA((7,)),
        ],
        out_shape=[jax.ShapeDtypeStruct((count, width), BF16)] * 2,
        compiler_params=params(63),
        cost_estimate=cost(60 * rows * count * width, 6 * rows * width),
        name="combine",
    )(routes_t, gates_t, home)
    kept = half // groups
    other = pl.pallas_call(
        other_kernel,
        in_specs=[smem, vmem],
        out_shape=jax.ShapeDtypeStruct((kept, early_sum.shape[1]), BF16),
        compiler_params=params(8),
        cost_estimate=cost(60 * rows * count * width, 4 * kept * width),
        name="other",
    )(which, early_sum)
    came_early = lax.ppermute(other, "expert", route)
    grad_weights = pl.pallas_call(
        functools.partial(join_kernel, early_cols, late_cols),
        in_specs=[smem, vmem, vmem, vmem],
        out_shape=jax.ShapeDtypeStruct((1, kept, 3 * ff), BF16),
        compiler_params=params(8),
        name="join",
    )(which, early_sum, came_early, late_sum)
    return (layer_out, grad_tokens, grad_weights)


def solution(mesh):
    placed = (
        P(("dp", "expert"), None),
        P(("dp", "expert"), None),
        P(("dp", "expert"), None),
        P(("dp", "expert"), None),
        P("expert", None, None),
    )
    return jax.shard_map(
        local,
        mesh=mesh,
        in_specs=placed,
        out_specs=(P(("dp", "expert"), None), P(("dp", "expert"), None), P("expert", "dp", None)),
        check_vma=False,
    )
```

```python
import functools

import jax
import jax.numpy as jnp
from jax import lax
from jax.experimental import pallas as pl
from jax.experimental.pallas import tpu as pltpu
from jax.sharding import PartitionSpec as P

BF16 = jnp.bfloat16
F32 = jnp.float32
CAP = 14
ROWS = 16
LANES = 128


def dot(a, b, dims):
    return lax.dot_general(a, b, (dims, ((), ())), preferred_element_type=F32)


def dispatch_mask(routes, slots):
    top, tokens = routes.shape
    slot = lax.broadcasted_iota(jnp.int32, (slots, tokens), 0)
    names = [routes[k : k + 1, :] == slot for k in range(top)]
    named = names[0]
    for one in names[1:]:
        named = named | one
    earlier = (
        lax.broadcasted_iota(jnp.int32, (tokens, tokens), 0)
        < lax.broadcasted_iota(jnp.int32, (tokens, tokens), 1)
    )
    place = dot(
        jnp.where(named, 1.0, 0.0).astype(BF16),
        jnp.where(earlier, 1.0, 0.0).astype(BF16),
        ((1,), (0,)),
    ).astype(jnp.int32)
    return names, jnp.where(named, place, ROWS)


def by_slot(place):
    at = lax.broadcasted_iota(jnp.int32, (place.shape[0], ROWS, place.shape[1]), 1)
    return place[:, None, :] == at


def by_place(place):
    at = lax.broadcasted_iota(jnp.int32, (CAP,) + place.shape, 0)
    return place[None, :, :] == at


def onehot(mask):
    return jnp.where(mask, 1.0, 0.0).astype(BF16)


def strip_rows(slots, columns):
    row = lax.broadcasted_iota(jnp.int32, (slots * ROWS, columns), 0)
    col = lax.broadcasted_iota(jnp.int32, (slots * ROWS, columns), 1)
    return onehot(row == (col % slots) * ROWS + CAP + col // slots)


def strip_picks(slots):
    row = lax.broadcasted_iota(jnp.int32, (2 * slots, slots * ROWS), 0)
    col = lax.broadcasted_iota(jnp.int32, (2 * slots, slots * ROWS), 1)
    return onehot(col == (row % slots) * ROWS + CAP + row // slots)


def to_strips(tail, slots):
    strips = [
        jnp.concatenate(
            [
                tail[j * slots : (j + 1) * slots, q * LANES : (q + 1) * LANES]
                for j in range(CAP)
            ],
            axis=1,
        )
        for q in range(2)
    ]
    return jnp.concatenate(strips, axis=0)


def from_strips(strips, slots):
    tails = [
        jnp.concatenate(
            [
                strips[q * slots : (q + 1) * slots, j * LANES : (j + 1) * LANES]
                for j in range(CAP)
            ],
            axis=0,
        )
        for q in range(2)
    ]
    return jnp.concatenate(tails, axis=1)


def slot_gates(names, gates):
    total = jnp.where(names[0], gates[0:1, :], 0.0)
    for k in range(1, len(names)):
        total = total + jnp.where(names[k], gates[k : k + 1, :], 0.0)
    return total


def pack_kernel(
    routes_hbm,
    gates_hbm,
    tokens_hbm,
    out_grad_hbm,
    send_hbm,
    routes_ref,
    gates_ref,
    tokens_ref,
    out_grad_ref,
    send_ref,
    in_sems,
    out_sems,
):
    slots, _, main = send_ref.shape
    pieces = out_sems.shape[0]
    step = main // pieces
    pairs = (
        (routes_hbm, routes_ref),
        (gates_hbm, gates_ref),
        (tokens_hbm, tokens_ref),
        (out_grad_hbm, out_grad_ref),
    )
    loads = [pltpu.make_async_copy(*pair, in_sems.at[i]) for i, pair in enumerate(pairs)]
    for load in loads:
        load.start()
    loads[0].wait()
    names, place = dispatch_mask(routes_ref[...], slots)
    mask, turned = by_slot(place), by_place(place)
    rows = slots * ROWS
    pick = jnp.concatenate([onehot(mask).reshape(rows, -1), strip_rows(slots, LANES)], axis=1)
    tail_pick = onehot(turned).reshape(CAP * slots, -1)
    loads[1].wait()
    weight = slot_gates(names, gates_ref[...])
    row_gate = jnp.sum(jnp.where(mask, weight[:, None, :], 0.0), axis=2, keepdims=True)
    row_gate = jnp.where(
        lax.broadcasted_iota(jnp.int32, row_gate.shape, 1) < CAP, row_gate, 1.0
    )
    tail_gate = jnp.sum(jnp.where(turned, weight[None, :, :], 0.0), axis=2, keepdims=True)
    tail_gate = tail_gate.reshape(CAP * slots, 1)
    loads[2].wait()
    loads[3].wait()
    x_tail = dot(tail_pick, tokens_ref[:, main:], ((1,), (0,)))
    dy_tail = dot(tail_pick, out_grad_ref[:, main:], ((1,), (0,))) * tail_gate
    blank = jnp.zeros((LANES - 2 * slots, main), BF16)
    x_strips = jnp.concatenate([to_strips(x_tail.astype(BF16), slots), blank], axis=0)
    dy_strips = jnp.concatenate([to_strips(dy_tail.astype(BF16), slots), blank], axis=0)
    stores = []
    for piece in range(pieces):
        at = slice(piece * step, (piece + 1) * step)
        cols = pl.ds(piece * step, step)
        source = jnp.concatenate([tokens_ref[:, at], x_strips[:, at]], axis=0)
        x = dot(pick, source, ((1,), (0,)))
        send_ref[:, :ROWS, cols] = x.astype(BF16).reshape(slots, ROWS, step)
        source = jnp.concatenate([out_grad_ref[:, at], dy_strips[:, at]], axis=0)
        g = dot(pick, source, ((1,), (0,))).reshape(slots, ROWS, step)
        send_ref[:, ROWS:, cols] = (row_gate * g).astype(BF16)
        stores.append(
            pltpu.make_async_copy(
                send_ref.at[:, :, cols], send_hbm.at[:, :, cols], out_sems.at[piece]
            )
        )
        stores[-1].start()
    for store in stores:
        store.wait()


def unpack_rows(rows_ref, begin, out_ref):
    slots, _, main = rows_ref.shape
    rows = slots * ROWS
    came = rows_ref[:, begin : begin + ROWS, :]
    live = lax.broadcasted_iota(jnp.int32, (1, ROWS, 1), 1) < CAP
    out_ref[:, :main] = jnp.where(live, came, jnp.zeros((), BF16)).reshape(rows, main)
    strips = dot(strip_picks(slots), came.reshape(rows, main), ((1,), (0,))).astype(BF16)
    row = lax.broadcasted_iota(jnp.int32, (rows, CAP * slots), 0)
    col = lax.broadcasted_iota(jnp.int32, (rows, CAP * slots), 1)
    turn = onehot(col == (row % ROWS) * slots + row // ROWS)
    out_ref[:, main:] = dot(turn, from_strips(strips, slots), ((1,), (0,))).astype(BF16)


def state_rows(a, b, e, qg_ref, qu_ref, h_ref):
    s = jax.nn.sigmoid(a)
    active = a * s
    h_ref[...] = (active * b).astype(BF16)
    qg_ref[...] = (e * b * s * (1.0 + a * (1.0 - s))).astype(BF16)
    qu_ref[...] = (e * active).astype(BF16)


def expert_rows(x_ref, dy_ref, g, u, v, qg_ref, qu_ref, h_ref):
    x = x_ref[...]
    a = dot(x, g, ((1,), (0,)))
    b = dot(x, u, ((1,), (0,)))
    e = dot(dy_ref[...], v, ((1,), (0,)))
    state_rows(a, b, e, qg_ref, qu_ref, h_ref)


def half_grads(x_ref, dy_ref, n, which, rhs):
    lhs_ref = dy_ref if n == 2 else x_ref
    half = lhs_ref.shape[1] // 2
    cols = pl.ds(pl.multiple_of(which * half, half), half)
    return dot(lhs_ref[:, cols], rhs, ((0,), (0,))).astype(BF16)


def early_kernel(
    plan,
    groups,
    which_ref,
    rows_ref,
    w_ref,
    partial_ref,
    qg_ref,
    qu_ref,
    h_ref,
    sent_ref,
    qg0_ref,
    qu0_ref,
    h0_ref,
    x_hbm,
    dy_hbm,
    x_ref,
    dy_ref,
    sems,
):
    width = x_ref.shape[1]
    block = width // 2 // groups
    all_refs = ((qg0_ref, qu0_ref, h0_ref), (qg_ref, qu_ref, h_ref))

    def copies():
        return [
            pltpu.make_async_copy(x_ref, x_hbm, sems.at[0]),
            pltpu.make_async_copy(dy_ref, dy_hbm, sems.at[1]),
        ]

    for step, (j, n) in enumerate(plan):

        @pl.when(pl.program_id(0) == step)
        def _(step=step, j=j, n=n):
            if step == 0:
                unpack_rows(rows_ref, 0, x_ref)
                unpack_rows(rows_ref, ROWS, dy_ref)
                for copy in copies():
                    copy.start()
            refs = all_refs[min(j, 1)]
            if n is None:
                chunk, ff = h_ref.shape[1], w_ref.shape[1] // 3
                begins = [n * ff + j * chunk for n in range(3)]
                weights = (w_ref[:, at : at + chunk] for at in begins)
                expert_rows(x_ref, dy_ref, *weights, *refs)
                return
            if j == 0:
                sent_ref[...] = half_grads(x_ref, dy_ref, n, 1 - which_ref[0], refs[n][...])
                return
            lhs_ref = dy_ref if n == 2 else x_ref
            value = dot(lhs_ref[...], refs[n][...], ((0,), (0,))).astype(BF16)
            for half in range(2):
                for d in range(groups):
                    old, new = (half * groups + d) * block, (2 * d + half) * block
                    partial_ref[new : new + block] = value[old : old + block]
            if step == len(plan) - 1:
                for copy in copies():
                    copy.wait()


def later_kernel(
    plan, which_ref, x_ref, dy_ref, qg_ref, qu_ref, h_ref, kept_ref, sent_ref, own_ref
):
    refs = (qg_ref, qu_ref, h_ref)
    for step, (j, n, out) in enumerate(plan):

        @pl.when(pl.program_id(0) == step)
        def _(j=j, n=n, out=out):
            rhs = refs[n][...] if j == 0 else kept_ref[...]
            which = which_ref[0] if out else 1 - which_ref[0]
            (sent_ref, own_ref)[out][...] = half_grads(x_ref, dy_ref, n, which, rhs)


def late_sum_kernel(own_ref, came_ref, out_ref):
    out_ref[...] = (own_ref[...].astype(F32) + came_ref[...].astype(F32)).astype(BF16)


def late_join_kernel(first_ref, own_ref, came_ref, out_ref):
    columns = came_ref.shape[1]
    out_ref[:, :columns] = first_ref[...]
    total = own_ref[...].astype(F32) + came_ref[...].astype(F32)
    out_ref[:, columns:] = total.astype(BF16)


def back_kernel(
    h0_ref, qg0_ref, qu0_ref, h_ref, qg_ref, qu_ref, w_ref, tail_ref, out_ref, strips_ref
):
    slots, _, block = out_ref.shape
    rows = slots * ROWS
    chunk = h0_ref.shape[1]
    ff = w_ref.shape[1] // 3
    at = pl.program_id(0)

    def product(first_ref, rest_ref, lines_ref, base):
        value = dot(first_ref[...], lines_ref[:, base : base + chunk], ((1,), (1,)))
        rest = lines_ref[:, base + chunk : base + ff]
        return value + dot(rest_ref[...], rest, ((1,), (1,)))

    def both(lines_ref):
        y = product(h0_ref, h_ref, lines_ref, 2 * ff)
        dx = product(qg0_ref, qg_ref, lines_ref, 0) + product(qu0_ref, qu_ref, lines_ref, ff)
        return y, dx

    @pl.when(at == 0)
    def _():
        row = lax.broadcasted_iota(jnp.int32, (CAP * slots, rows), 0)
        col = lax.broadcasted_iota(jnp.int32, (CAP * slots, rows), 1)
        turn = onehot(col == (row % slots) * ROWS + row // slots)
        for i, value in enumerate(both(tail_ref)):
            tail = dot(turn, value.astype(BF16), ((1,), (0,))).astype(BF16)
            strips = to_strips(tail, slots)
            for p in range(strips_ref.shape[0]):
                strips_ref[p, i] = strips[:, p * block : (p + 1) * block]

    spread = strip_rows(slots, 2 * slots)
    for i, value in enumerate(both(w_ref)):
        value = value.astype(BF16).astype(F32) + dot(spread, strips_ref[at, i], ((1,), (0,)))
        out_ref[:, i * ROWS : (i + 1) * ROWS, :] = value.astype(BF16).reshape(slots, ROWS, block)


def combine_kernel(routes_ref, gates_ref, back_hbm, layer_ref, grad_ref, back_ref, sems):
    slots, _, main = back_ref.shape
    rows = slots * ROWS
    count = layer_ref.shape[0]
    step = main // sems.shape[0]
    loads = []
    for c in range(0, main, step):
        cols = pl.ds(c, step)
        loads.append(
            pltpu.make_async_copy(
                back_hbm.at[:, :, cols], back_ref.at[:, :, cols], sems.at[c // step]
            )
        )
        loads[-1].start()
    names, place = dispatch_mask(routes_ref[...], slots)
    weight = slot_gates(names, gates_ref[...])

    def split(gate):
        high = gate.astype(BF16)
        return [high, (gate - high.astype(F32)).astype(BF16)]

    def turned_rows(mask, value):
        return jnp.where(mask, value, 0.0).reshape(-1, value.shape[-1]).T

    mask, turned = by_slot(place), by_place(place)
    take = strip_picks(slots)
    y_pick = jnp.concatenate(split(turned_rows(mask, weight[:, None, :])) + [take], axis=0)
    dx_pick = turned_rows(mask, jnp.ones((1, 1, count), F32)).astype(BF16)
    dx_pick = jnp.concatenate([dx_pick, take], axis=0)
    y_strips, dx_strips = [], []
    for c in range(0, main, step):
        cols = slice(c, c + step)
        loads[c // step].wait()
        y = dot(y_pick, back_ref[:, :ROWS, cols].reshape(rows, step), ((1,), (0,)))
        layer_ref[:, cols] = (y[:count] + y[count : 2 * count]).astype(BF16)
        y_strips.append(y[2 * count :].astype(BF16))
        dx = dot(dx_pick, back_ref[:, ROWS:, cols].reshape(rows, step), ((1,), (0,)))
        grad_ref[:, cols] = dx[:count].astype(BF16)
        dx_strips.append(dx[count:].astype(BF16))
    high, low = split(turned_rows(turned, weight[None, :, :]))
    y = from_strips(jnp.concatenate(y_strips, axis=1), slots)
    value = dot(high, y, ((1,), (0,))) + dot(low, y, ((1,), (0,)))
    layer_ref[:, main:] = value.astype(BF16)
    pick = turned_rows(turned, jnp.ones((1, 1, count), F32)).astype(BF16)
    dx = from_strips(jnp.concatenate(dx_strips, axis=1), slots)
    grad_ref[:, main:] = dot(pick, dx, ((1,), (0,))).astype(BF16)


def other_kernel(which_ref, summed_ref, out_ref):
    half = out_ref.shape[0]
    begin = pl.multiple_of((1 - which_ref[0]) * half, half)
    out_ref[...] = summed_ref[pl.ds(begin, half), :]


def join_kernel(early_plan, late_plan, which_ref, early_ref, came_ref, late_ref, out_ref):
    half, columns = came_ref.shape
    chunk = columns // len(early_plan)
    steps = out_ref.shape[2] // 3 // chunk
    own = early_ref[pl.ds(pl.multiple_of(which_ref[0] * half, half), half), :]
    total = (own.astype(F32) + came_ref[...].astype(F32)).astype(BF16)
    for plan, value in ((early_plan, total), (late_plan, late_ref[...])):
        for i, (j, n) in enumerate(plan):
            new = (n * steps + j) * chunk
            out_ref[0, :, new : new + chunk] = value[:, i * chunk : (i + 1) * chunk]


def params(mib):
    return pltpu.CompilerParams(vmem_limit_bytes=int(mib * 1024 * 1024))


def cost(flops, moved):
    return pl.CostEstimate(flops=flops, bytes_accessed=moved, transcendentals=0)


def local(tokens, out_grad, routes, gates, weights):
    slots = lax.axis_size("expert")
    groups = lax.axis_size("dp")
    count, width = tokens.shape
    top = routes.shape[1]
    weight = weights[0]
    ff = weight.shape[1] // 3
    rows = slots * ROWS
    chunk = 256
    steps = ff // chunk
    half = width // 2
    routes_t = routes.T
    gates_t = gates.T
    upper = (lax.axis_index("expert") >= slots // 2).astype(jnp.int32)
    which = upper.reshape(1)
    smem = pl.BlockSpec(memory_space=pltpu.SMEM)
    vmem = pl.BlockSpec(memory_space=pltpu.VMEM)
    main = width - 2 * LANES
    pair = pltpu.HBM((slots, 2 * ROWS, main), BF16)
    flat = pltpu.HBM((rows, width), BF16)
    hbm = pl.BlockSpec(memory_space=pltpu.HBM)
    sent = pl.pallas_call(
        pack_kernel,
        in_specs=[hbm] * 4,
        out_specs=hbm,
        out_shape=pair,
        scratch_shapes=[
            pltpu.VMEM((top, count), jnp.int32),
            pltpu.VMEM((top, count), F32),
            pltpu.VMEM((count, width), BF16),
            pltpu.VMEM((count, width), BF16),
            pltpu.VMEM((slots, 2 * ROWS, main), BF16),
            pltpu.SemaphoreType.DMA((4,)),
            pltpu.SemaphoreType.DMA((7,)),
        ],
        compiler_params=params(54.2),
        cost_estimate=cost(4 * rows * count * width, 6 * rows * width),
        name="pack",
    )(routes_t, gates_t, tokens, out_grad)
    sent, which = lax.optimization_barrier((sent, which))
    came = lax.all_to_all(sent, "expert", split_axis=0, concat_axis=0, tiled=True)

    early_plan = ((0, None), (0, 0), (0, 1), (1, None), (1, 0), (1, 1))
    early_plan += ((2, None), (2, 0), (2, 1), (2, 2))
    early_cols = tuple(one for one in early_plan if one[0] > 0 and one[1] is not None)
    late_cols = ((0, 0), (0, 1), (0, 2), (1, 2))
    state = pltpu.HBM((rows, ff - chunk), BF16)
    state_spec = pl.BlockSpec((rows, chunk), lambda p: (0, jnp.where(p >= 6, 1, 0)))
    first_state = pltpu.HBM((rows, chunk), BF16)
    first_spec = pl.BlockSpec((rows, chunk), lambda p: (0, 0))
    sent_shape = pltpu.HBM((half, 2 * chunk), BF16)
    early, qg, qu, h, sent_first, qg0, qu0, h0, x, dy = pl.pallas_call(
        functools.partial(early_kernel, early_plan, groups),
        grid=(len(early_plan),),
        in_specs=[smem, vmem, vmem],
        out_specs=[
            pl.BlockSpec(
                (width, chunk), lambda p: (0, jnp.maximum(p - 4 - jnp.where(p > 6, 1, 0), 0))
            )
        ]
        + [state_spec] * 3
        + [pl.BlockSpec((half, chunk), lambda p: (0, jnp.clip(p - 1, 0, 1)))]
        + [first_spec] * 3
        + [hbm] * 2,
        out_shape=[pltpu.HBM((width, len(early_cols) * chunk), BF16)]
        + [state] * 3
        + [sent_shape]
        + [first_state] * 3
        + [flat] * 2,
        scratch_shapes=[
            pltpu.VMEM((rows, width), BF16),
            pltpu.VMEM((rows, width), BF16),
            pltpu.SemaphoreType.DMA((2,)),
        ],
        compiler_params=params(27),
        cost_estimate=cost(8 * rows * width * ff, 16 * width * ff),
        name="early_grads",
    )(which, came, weight)
    early_sum = lax.psum_scatter(early, "dp", scatter_dimension=0, tiled=True)
    flat_spec = pl.BlockSpec((rows, width), lambda p: (0, 0))
    route = [((i + slots // 2) % slots, i) for i in range(slots)]
    came_first = lax.ppermute(sent_first, "expert", route)
    plan = ((0, 2, 0), (1, 2, 0), (0, 0, 1), (0, 1, 1), (0, 2, 1), (1, 2, 1))
    sent_second, own = pl.pallas_call(
        functools.partial(later_kernel, plan),
        grid=(len(plan),),
        in_specs=[smem, flat_spec, flat_spec] + [first_spec] * 4,
        out_specs=[
            pl.BlockSpec((half, chunk), lambda p: (0, jnp.minimum(p, 1))),
            pl.BlockSpec((half, chunk), lambda p: (0, jnp.maximum(p - 2, 0))),
        ],
        out_shape=[sent_shape, pltpu.HBM((half, len(late_cols) * chunk), BF16)],
        compiler_params=params(63),
        cost_estimate=cost(2 * rows * width * ff, 8 * width * ff),
        name="later_grads",
    )(which, x, dy, qg0, qu0, h0, h)
    came_second = lax.ppermute(sent_second, "expert", route)
    block = main // 2
    back = pl.pallas_call(
        back_kernel,
        grid=(main // block,),
        in_specs=[pl.BlockSpec((rows, chunk), lambda j: (0, 0))] * 3
        + [pl.BlockSpec((rows, ff - chunk), lambda j: (0, 0))] * 3
        + [
            pl.BlockSpec((block, 3 * ff), lambda j: (j, 0)),
            pl.BlockSpec((2 * LANES, 3 * ff), lambda j: (main // (2 * LANES), 0)),
        ],
        out_specs=pl.BlockSpec((slots, 2 * ROWS, block), lambda j: (0, 0, j)),
        out_shape=pair,
        scratch_shapes=[pltpu.VMEM((main // block, 2, 2 * slots, block), BF16)],
        compiler_params=params(63),
        cost_estimate=cost(6 * rows * width * ff, 12 * width * ff),
        name="back",
    )(h0, qg0, qu0, h, qg, qu, weight, weight)
    home = lax.all_to_all(back, "expert", split_axis=0, concat_axis=0, tiled=True)
    lines = half // 4
    part_spec = pl.BlockSpec((lines, 2 * chunk), lambda p: (p, 0))
    late_first = pl.pallas_call(
        late_sum_kernel,
        grid=(4,),
        in_specs=[part_spec] * 2,
        out_specs=part_spec,
        out_shape=sent_shape,
        compiler_params=params(63),
        cost_estimate=cost(60 * rows * count * width, 16 * half * chunk),
        name="late_sum",
    )(own, came_first)
    late = pl.pallas_call(
        late_join_kernel,
        grid=(4,),
        in_specs=[part_spec, pl.BlockSpec((lines, 2 * chunk), lambda p: (p, 1)), part_spec],
        out_specs=pl.BlockSpec((lines, 4 * chunk), lambda p: (p, 0)),
        out_shape=pltpu.HBM((half, 4 * chunk), BF16),
        compiler_params=params(63),
        cost_estimate=cost(half * 4 * chunk, 24 * half * chunk),
        name="late_join",
    )(late_first, own, came_second)
    late_sum = lax.psum_scatter(late, "dp", scatter_dimension=0, tiled=True)
    layer_out, grad_tokens = pl.pallas_call(
        combine_kernel,
        in_specs=[vmem, vmem, hbm],
        scratch_shapes=[
            pltpu.VMEM((slots, 2 * ROWS, main), BF16),
            pltpu.SemaphoreType.DMA((7,)),
        ],
        out_shape=[jax.ShapeDtypeStruct((count, width), BF16)] * 2,
        compiler_params=params(63),
        cost_estimate=cost(60 * rows * count * width, 6 * rows * width),
        name="combine",
    )(routes_t, gates_t, home)
    kept = half // groups
    other = pl.pallas_call(
        other_kernel,
        in_specs=[smem, vmem],
        out_shape=jax.ShapeDtypeStruct((kept, early_sum.shape[1]), BF16),
        compiler_params=params(8),
        cost_estimate=cost(60 * rows * count * width, 4 * kept * width),
        name="other",
    )(which, early_sum)
    came_early = lax.ppermute(other, "expert", route)
    grad_weights = pl.pallas_call(
        functools.partial(join_kernel, early_cols, late_cols),
        in_specs=[smem, vmem, vmem, vmem],
        out_shape=jax.ShapeDtypeStruct((1, kept, 3 * ff), BF16),
        compiler_params=params(8),
        name="join",
    )(which, early_sum, came_early, late_sum)
    return (layer_out, grad_tokens, grad_weights)


def solution(mesh):
    placed = (
        P(("dp", "expert"), None),
        P(("dp", "expert"), None),
        P(("dp", "expert"), None),
        P(("dp", "expert"), None),
        P("expert", None, None),
    )
    return jax.shard_map(
        local,
        mesh=mesh,
        in_specs=placed,
        out_specs=(P(("dp", "expert"), None), P(("dp", "expert"), None), P("expert", "dp", None)),
        check_vma=False,
    )
```
